128 devices in a mesh: dp: 4 (over x), seq: 4 (over y_hi, core), tensor: 8 (over z, y_lo).
Axes of the slice: x: 4, y: 4 (y_hi: 2, y_lo: 2; y = y_hi * 2 + y_lo), z: 4, core: 2. Of those that a mesh axis runs over, the one named last changes fastest.
Arguments:
- encoder_out: bfloat16 [4, 1024, 4096], P('dp', 'seq', 'tensor'), may hold values from -6 to 6
- w_key: bfloat16 [2, 4096, 4096], P(None, None, 'tensor'), may hold values from -0.09375 to 0.09375
- w_value: bfloat16 [2, 4096, 4096], P(None, None, 'tensor'), may hold values from -0.09375 to 0.09375
- queries: bfloat16 [2, 4, 512, 4096], P(None, 'dp', 'seq', 'tensor'), may hold values from -140 to 140
- grad_context: bfloat16 [2, 4, 512, 4096], P(None, 'dp', 'seq', 'tensor'), may hold values from -6 to 6
Outputs:
- grad_queries: bfloat16 [2, 4, 512, 4096], P(None, 'dp', 'seq', 'tensor')
- grad_encoder: bfloat16 [4, 1024, 4096], P('dp', 'seq', 'tensor')
- grad_w_key: bfloat16 [2, 4096, 4096], P(None, ('dp', 'seq'), 'tensor')
- grad_w_value: bfloat16 [2, 4096, 4096], P(None, ('dp', 'seq'), 'tensor')
The draws below stay inside these ranges and needn't reach their ends.
All inputs are finite; a program needn't handle non-finite values.
Results may differ from the reference program's by a relative error of at most 0.035.
The reference program's roundings to bfloat16 on the way (of `probs_low` and `dscores`) count: a program that leaves them out, or rounds other values in their place, can miss the bound.
Values may be sent and summed in bfloat16 or wider, within the bound.
No kernel may reach another device: no remote copies, remote signals or barrier semaphores. Data moves between devices by JAX's collectives and lax.ppermute only.
A program may use at most 128 MiB of HBM per device.

```python
import jax
import jax.numpy as jnp
from jax import lax

D = 4096
HEADS = 16
DH = 256
LAYERS = 2
B_DEV = 1
SE_DEV = 256
SQ_DEV = 128
BATCH = 4
SE = 1024
SQ = 512
HDIM = 4096
N_DP = 4
N_SEQ = 4


def draw_queries(key, part):
    key = jax.random.fold_in(key, 7)
    second = jax.random.fold_in(key, 1)
    shape = (LAYERS, BATCH, SQ, HEADS * DH)
    samples = jnp.clip(jax.random.normal(second, shape, jnp.float32), -5.0, 5.0)
    return samples.astype(jnp.bfloat16)


def levels(stream_key, extent, cuts, least, largest):
    def one(dim, shards_of):
        heights = jax.random.uniform(jax.random.fold_in(jax.random.fold_in(stream_key, 6), dim), (shards_of,), jnp.float32, least / len(cuts), largest / len(cuts))
        return jnp.repeat(jnp.exp(heights), extent[dim] // shards_of).reshape((-1,) + (1,) * (len(extent) - dim - 1))

    level = one(*cuts[0])
    for cut in cuts[1:]:
        level = level * one(*cut)
    return level


def gaussian(own_key, dims, deviation, limit, cuts=(), held_as=jnp.bfloat16):
    factor_of = levels(own_key, dims, cuts, -0.22, 0.18) if cuts else 1.0
    result = jax.random.normal(own_key, dims, jnp.float32) * deviation * factor_of
    return jnp.minimum(jnp.maximum(result, -limit), limit).astype(held_as)


def setup_inputs(seed: int = 0) -> dict:
    splits = jax.random.split(jax.random.key(seed), 6)
    encoder_out = gaussian(splits[0], (BATCH, SE, D), 1.0, 6.0, ((0, 4), (1, 4), (2, 8)))
    w_key = gaussian(splits[1], (LAYERS, D, HDIM), D ** -0.5, 0.09375, ((2, 8),))
    w_value = gaussian(splits[2], (LAYERS, D, HDIM), D ** -0.5, 0.09375, ((2, 8),))
    queries = draw_queries(jax.random.fold_in(splits[5], 71), 0)
    grad_context = gaussian(splits[4], (LAYERS, BATCH, SQ, HDIM), 1.0, 6.0, ((1, 4), (2, 4), (3, 8)))
    return {"encoder_out": encoder_out, "w_key": w_key, "w_value": w_value, "queries": queries, "grad_context": grad_context}


def attend_block(keys, values, query_block, grad_block):
    scale = DH ** -0.5
    scores = jnp.einsum('bqhe,bkhe->bhqk', query_block.astype(jnp.float32), keys.astype(jnp.float32)) * scale
    probs = jax.nn.softmax(scores, axis=-1)
    dprobs = jnp.einsum('bqhe,bkhe->bhqk', grad_block.astype(jnp.float32), values.astype(jnp.float32))
    delta = jnp.sum(probs * dprobs, axis=-1, keepdims=True)
    dscores = (probs * (dprobs - delta) * scale).astype(jnp.bfloat16)
    probs_low = probs.astype(jnp.bfloat16)
    grad_q = jnp.einsum('bhqk,bkhe->bqhe', dscores.astype(jnp.float32), keys.astype(jnp.float32)).astype(jnp.bfloat16)
    grad_k = jnp.einsum('bhqk,bqhe->bkhe', dscores.astype(jnp.float32), query_block.astype(jnp.float32)).astype(jnp.bfloat16)
    grad_v = jnp.einsum('bhqk,bqhe->bkhe', probs_low.astype(jnp.float32), grad_block.astype(jnp.float32)).astype(jnp.bfloat16)
    return grad_q, grad_k, grad_v


def reference(encoder_out, w_key, w_value, queries, grad_context):
    flat_enc = encoder_out.reshape(BATCH * SE, D)
    enc_blocks = encoder_out.reshape(N_DP, B_DEV, N_SEQ, SE_DEV, D).transpose(0, 2, 1, 3, 4).reshape(N_DP * N_SEQ, B_DEV * SE_DEV, D)
    grad_enc = jnp.zeros((BATCH * SE, D), jnp.float32)
    grad_q_all = []
    grad_wk_all = []
    grad_wv_all = []
    for layer in range(LAYERS):
        keys = jnp.dot(flat_enc, w_key[layer], preferred_element_type=jnp.float32).astype(jnp.bfloat16)
        values = jnp.dot(flat_enc, w_value[layer], preferred_element_type=jnp.float32).astype(jnp.bfloat16)
        keys4 = keys.reshape(BATCH, SE, HEADS, DH)
        values4 = values.reshape(BATCH, SE, HEADS, DH)
        query_blocks = queries[layer].reshape(BATCH, N_SEQ, SQ_DEV, HEADS, DH).transpose(1, 0, 2, 3, 4)
        grad_blocks = grad_context[layer].reshape(BATCH, N_SEQ, SQ_DEV, HEADS, DH).transpose(1, 0, 2, 3, 4)
        grad_qs, grad_ks, grad_vs = lax.map(lambda pair: attend_block(keys4, values4, pair[0], pair[1]), (query_blocks, grad_blocks))
        grad_q_all.append(grad_qs.transpose(1, 0, 2, 3, 4).reshape(BATCH, SQ, HDIM))
        grad_keys = jnp.sum(grad_ks.astype(jnp.float32), axis=0).astype(jnp.bfloat16).reshape(BATCH * SE, HDIM)
        grad_values = jnp.sum(grad_vs.astype(jnp.float32), axis=0).astype(jnp.bfloat16).reshape(BATCH * SE, HDIM)
        grad_enc = grad_enc + jnp.dot(grad_keys, w_key[layer].T, preferred_element_type=jnp.float32) + jnp.dot(grad_values, w_value[layer].T, preferred_element_type=jnp.float32)
        joined = jnp.concatenate([grad_keys, grad_values], axis=1)
        joined_blocks = joined.reshape(N_DP, B_DEV, N_SEQ, SE_DEV, 2 * HDIM).transpose(0, 2, 1, 3, 4).reshape(N_DP * N_SEQ, B_DEV * SE_DEV, 2 * HDIM)

        def add_block(total, pair):
            term = jnp.dot(pair[0].T, pair[1], preferred_element_type=jnp.float32)
            return total + term.astype(jnp.bfloat16).astype(jnp.float32), None

        total, unused = lax.scan(add_block, jnp.zeros((D, 2 * HDIM), jnp.float32), (enc_blocks, joined_blocks))
        grad_wk_all.append(total[:, :HDIM].astype(jnp.bfloat16))
        grad_wv_all.append(total[:, HDIM:].astype(jnp.bfloat16))
    grad_queries = jnp.stack(grad_q_all)
    grad_encoder = grad_enc.reshape(BATCH, SE, D).astype(jnp.bfloat16)
    return grad_queries, grad_encoder, jnp.stack(grad_wk_all), jnp.stack(grad_wv_all)
```

```python
import functools

import jax
import jax.numpy as jnp
from jax import lax
from jax.experimental import pallas as pl
from jax.experimental.pallas import tpu as pltpu
from jax.sharding import PartitionSpec as P

DH = 256
BF = jnp.bfloat16
F32 = jnp.float32
NT = (((1,), (1,)), ((), ()))
TN = (((0,), (0,)), ((), ()))
MB = 1024 * 1024


def params(mb):
    return pltpu.CompilerParams(vmem_limit_bytes=mb * MB)


def cost(flops, nbytes):
    return pl.CostEstimate(flops=flops, bytes_accessed=nbytes, transcendentals=0)


def swap_core(x):
    return lax.ppermute(x, "seq", [(s, s ^ 1) for s in range(4)])


def swap_yhi(x):
    return lax.ppermute(x, "seq", [(s, s ^ 2) for s in range(4)])


def swap_ylo(x):
    return lax.ppermute(x, "tensor", [(t, t ^ 1) for t in range(8)])


def swap_x(x, m):
    return lax.ppermute(x, "dp", [(d, d ^ m) for d in range(4)])


def swap_z(x, m):
    return lax.ppermute(x, "tensor", [(t, t ^ (2 * m)) for t in range(8)])


def shift_z(x, k):
    return lax.ppermute(x, "tensor", [(t, (t + 2 * k) % 8) for t in range(8)])


def shift_y(x, k):
    pairs = []
    for s in range(4):
        for t in range(8):
            y = ((s // 2) * 2 + t % 2 + k) % 4
            pairs.append((s * 8 + t, ((y // 2) * 2 + s % 2) * 8 + (t // 2) * 2 + y % 2))
    return lax.ppermute(x, ("seq", "tensor"), pairs)


def place(idx, k, j, first):
    y = idx[5]
    z = idx[3]
    if first:
        yy, zz = lax.rem(y + 4 - j, 4), lax.rem(z + 4 - k, 4)
    else:
        yy, zz = lax.rem(y + 4 - k, 4), lax.rem(z + 4 - j, 4)
    hh = lax.div(yy, 2)
    tt = zz * 2 + lax.rem(yy, 2)
    return hh, tt


def project_body(idx, *refs):
    pieces = refs[:8]
    wk, wv, send, keep, enc, acc = refs[8:]
    i = pl.program_id(0)
    c = idx[1]

    @pl.when(i == 0)
    def _():
        for half in range(2):
            for k in range(4):
                for j in range(4):
                    hh, tt = place(idx, k, j, half == 0)
                    rows = pl.ds(pl.multiple_of(hh * 256, 256), 256)
                    chunk = lax.div(tt, 2)
                    cols = pl.ds(
                        pl.multiple_of(lax.rem(tt, 2) * 512 + half * 256, 256), 256
                    )
                    enc[chunk, rows, cols] = pieces[half * 4 + k][j]
        acc[...] = jnp.zeros_like(acc)

    e = enc[i]
    acc[:, :512] += jnp.dot(e, wk[0], preferred_element_type=F32)
    acc[:, 512:] += jnp.dot(e, wv[0], preferred_element_type=F32)

    @pl.when(i == 3)
    def _():
        mine = pl.multiple_of(c * 256, 256)
        other = pl.multiple_of((1 - c) * 256, 256)
        keep[:, :256] = acc[:, pl.ds(mine, 256)].astype(BF)
        keep[:, 256:] = acc[:, pl.ds(mine + 512, 256)].astype(BF)
        send[:, :256] = acc[:, pl.ds(other, 256)].astype(BF)
        send[:, 256:] = acc[:, pl.ds(other + 512, 256)].astype(BF)


def project(idx, pieces, w_key, w_value):
    whole = pl.BlockSpec((4, 256, 256), lambda i, idx: (0, 0, 0))
    wspec = pl.BlockSpec((1, 1024, 512), lambda i, idx: (idx[0], i, 0))
    out = pl.BlockSpec((512, 512), lambda i, idx: (0, 0))
    return pl.pallas_call(
        project_body,
        grid_spec=pltpu.PrefetchScalarGridSpec(
            num_scalar_prefetch=1,
            grid=(4,),
            in_specs=[whole] * 8 + [wspec, wspec],
            out_specs=[out, out],
            scratch_shapes=[pltpu.VMEM((4, 512, 1024), BF), pltpu.VMEM((512, 1024), F32)],
        ),
        out_shape=[jax.ShapeDtypeStruct((512, 512), BF)] * 2,
        compiler_params=params(32),
        cost_estimate=cost(2 * 512 * 4096 * 1024, 14 * MB),
        name="project",
    )(idx, *pieces, w_key, w_value)


def sort_body(idx, *refs):
    pieces = refs[:8]
    keep, send = refs[8:]
    c = idx[1]
    for half in range(2):
        for k in range(4):
            for j in range(4):
                hh, tt = place(idx, k, j, half == 0)
                rows = pl.ds(pl.multiple_of(hh * 256, 256), 256)
                cols = pl.ds(pl.multiple_of(tt * 256, 256), 256)
                piece = pieces[half * 4 + k]

                @pl.when(c == half)
                def _():
                    keep[rows, cols] = piece[j]

                @pl.when(c != half)
                def _():
                    send[rows, cols] = piece[j]


def sort_pieces(idx, pieces):
    whole = pl.BlockSpec((4, 256, 256), lambda i, idx: (0, 0, 0))
    out = pl.BlockSpec((512, 2048), lambda i, idx: (0, 0))
    return pl.pallas_call(
        sort_body,
        grid_spec=pltpu.PrefetchScalarGridSpec(
            num_scalar_prefetch=1, grid=(1,), in_specs=[whole] * 8, out_specs=[out, out]
        ),
        out_shape=[jax.ShapeDtypeStruct((512, 2048), BF)] * 2,
        compiler_params=params(24),
        cost_estimate=cost(0, 8 * MB),
        name="sort_pieces",
    )(idx, *pieces)


def attend_body(kv_own, kv_oth, qg_own, qg_oth, gk, gv, gq, gk_acc, gv_acc):
    scale = DH ** (-0.5)
    gk_acc[...] = jnp.zeros_like(gk_acc)
    gv_acc[...] = jnp.zeros_like(gv_acc)
    for block in range(4):
        src = (qg_own, qg_oth)[block // 2]
        q = src[block % 2, 0]
        g = src[block % 2, 1]
        s = [
            lax.dot_general(kv[:, :256], q, NT, preferred_element_type=F32) * scale
            for kv in (kv_own, kv_oth)
        ]
        top = jnp.maximum(
            jnp.max(s[0], axis=0, keepdims=True), jnp.max(s[1], axis=0, keepdims=True)
        )
        p = [jnp.exp(part - top) for part in s]
        total = jnp.sum(p[0], axis=0, keepdims=True) + jnp.sum(p[1], axis=0, keepdims=True)
        p = [part / total for part in p]
        dp = [
            lax.dot_general(kv[:, 256:], g, NT, preferred_element_type=F32)
            for kv in (kv_own, kv_oth)
        ]
        delta = jnp.sum(p[0] * dp[0], axis=0, keepdims=True) + jnp.sum(
            p[1] * dp[1], axis=0, keepdims=True
        )
        ds = [(a * (b - delta) * scale).astype(BF) for a, b in zip(p, dp)]
        low = [a.astype(BF) for a in p]
        total_q = jnp.zeros((128, 256), F32)
        for part, kv in enumerate((kv_own, kv_oth)):
            rows = slice(part * 512, part * 512 + 512)
            gv_acc[rows] += jnp.dot(low[part], g, preferred_element_type=F32).astype(BF).astype(F32)
            gk_acc[rows] += jnp.dot(ds[part], q, preferred_element_type=F32).astype(BF).astype(F32)
            total_q += lax.dot_general(ds[part], kv[:, :256], TN, preferred_element_type=F32)
        gq[block] = total_q.astype(BF)
    gk[...] = gk_acc[...].astype(BF)
    gv[...] = gv_acc[...].astype(BF)


def attend(kv_own, kv_oth, qg_own, qg_oth):
    return pl.pallas_call(
        attend_body,
        out_shape=[
            jax.ShapeDtypeStruct((1024, 256), BF),
            jax.ShapeDtypeStruct((1024, 256), BF),
            jax.ShapeDtypeStruct((4, 128, 256), BF),
        ],
        scratch_shapes=[pltpu.VMEM((1024, 256), F32)] * 2,
        compiler_params=params(24),
        cost_estimate=cost(10 * 512 * 1024 * 256, 4 * MB),
        name="attend",
    )(kv_own, kv_oth, qg_own, qg_oth)


def weights_body(idx, ta, tb, ea, oa, eb, ob, kc, ko, vc, vo, out_a, out_b):
    c = idx[1]
    mine = pl.multiple_of(c * 256, 256)
    other = pl.multiple_of((1 - c) * 256, 256)
    for e, o, out in ((ea, oa, out_a), (eb, ob, out_b)):
        e1 = e[...]
        o1 = o[...]
        for base, gc, go in ((0, kc, ko), (512, vc, vo)):
            left = lax.dot_general(e1, gc[:512], TN, preferred_element_type=F32)
            left += lax.dot_general(o1, gc[512:], TN, preferred_element_type=F32)
            right = lax.dot_general(e1, go[512:], TN, preferred_element_type=F32)
            right += lax.dot_general(o1, go[:512], TN, preferred_element_type=F32)
            out[0, :, pl.ds(mine + base, 256)] = left.astype(out.dtype)
            out[0, :, pl.ds(other + base, 256)] = right.astype(out.dtype)


def weight_grads(idx, ta, tb, e_keep, e_oth, kc, ko, vc, vo, dtype):
    at_a = pl.BlockSpec((512, 256), lambda i, idx, ta, tb: (0, ta[i]))
    at_b = pl.BlockSpec((512, 256), lambda i, idx, ta, tb: (0, tb[i]))
    whole = pl.BlockSpec((1024, 256), lambda i, idx, ta, tb: (0, 0))
    out = pl.BlockSpec((1, 256, 1024), lambda i, idx, ta, tb: (i, 0, 0))
    return pl.pallas_call(
        weights_body,
        grid_spec=pltpu.PrefetchScalarGridSpec(
            num_scalar_prefetch=3,
            grid=(2,),
            in_specs=[at_a, at_a, at_b, at_b] + [whole] * 4,
            out_specs=[out, out],
        ),
        out_shape=[jax.ShapeDtypeStruct((2, 256, 1024), dtype)] * 2,
        compiler_params=params(24),
        cost_estimate=cost(2 * 1024 * 1024 * 1024, 6 * MB),
        name="weight_grads",
    )(idx, ta, tb, e_keep, e_oth, e_keep, e_oth, kc, ko, vc, vo)


def encoder_body(idx, ta, tb, *refs):
    g_own = refs[0:4]
    g_recv = refs[4]
    weights = (refs[5:9], refs[9:13])
    outs = refs[13:15]
    c = idx[1]
    mine = pl.ds(pl.multiple_of(c * 256, 256), 256)
    other = pl.ds(pl.multiple_of((1 - c) * 256, 256), 256)
    for (wk0, wv0, wk1, wv1), out in zip(weights, outs):
        total = lax.dot_general(g_own[0][...], wk0[0, :, mine], NT, preferred_element_type=F32)
        total += lax.dot_general(g_own[1][...], wk0[0, :, other], NT, preferred_element_type=F32)
        total += lax.dot_general(g_own[2][...], wv0[0, :, mine], NT, preferred_element_type=F32)
        total += lax.dot_general(g_own[3][...], wv0[0, :, other], NT, preferred_element_type=F32)
        total += lax.dot_general(g_recv[0], wk1[0, :, mine], NT, preferred_element_type=F32)
        total += lax.dot_general(g_recv[1], wk1[0, :, other], NT, preferred_element_type=F32)
        total += lax.dot_general(g_recv[2], wv1[0, :, mine], NT, preferred_element_type=F32)
        total += lax.dot_general(g_recv[3], wv1[0, :, other], NT, preferred_element_type=F32)
        out[0] = total.astype(out.dtype)


def encoder_grads(idx, ta, tb, kc, ko, vc, vo, g_recv, w_key, w_value, dtype):
    first = pl.BlockSpec((256, 256), lambda i, idx, ta, tb: (idx[0], 0))
    second = pl.BlockSpec((256, 256), lambda i, idx, ta, tb: (idx[0] + 2, 0))
    recv = pl.BlockSpec((4, 256, 256), lambda i, idx, ta, tb: (0, 0, 0))
    own_a = pl.BlockSpec((1, 512, 512), lambda i, idx, ta, tb: (idx[0], ta[i], 0))
    oth_a = pl.BlockSpec((1, 512, 512), lambda i, idx, ta, tb: (1 - idx[0], ta[i], 0))
    own_b = pl.BlockSpec((1, 512, 512), lambda i, idx, ta, tb: (idx[0], tb[i], 0))
    oth_b = pl.BlockSpec((1, 512, 512), lambda i, idx, ta, tb: (1 - idx[0], tb[i], 0))
    out = pl.BlockSpec((1, 256, 512), lambda i, idx, ta, tb: (i, 0, 0))
    return pl.pallas_call(
        encoder_body,
        grid_spec=pltpu.PrefetchScalarGridSpec(
            num_scalar_prefetch=3,
            grid=(2,),
            in_specs=[first, second, first, second, recv]
            + [own_a, own_a, oth_a, oth_a, own_b, own_b, oth_b, oth_b],
            out_specs=[out, out],
        ),
        out_shape=[jax.ShapeDtypeStruct((2, 256, 512), dtype)] * 2,
        compiler_params=params(32),
        cost_estimate=cost(2 * 256 * 2048 * 2048, 10 * MB),
        name="encoder_grads",
    )(
        idx, ta, tb, kc, ko, vc, vo, g_recv,
        w_key, w_value, w_key, w_value, w_key, w_value, w_key, w_value,
    )


def pick(x, index):
    return lax.dynamic_index_in_dim(x, index, 0, keepdims=False)


def on_device(encoder_out, w_key, w_value, queries, grad_context):
    d = lax.axis_index("dp")
    seq = lax.axis_index("seq")
    tensor = lax.axis_index("tensor")
    h, c = seq // 2, seq % 2
    z, yl = tensor // 2, tensor % 2
    idx = jnp.stack([h, c, d, z, yl, h * 2 + yl]).astype(jnp.int32)

    enc = encoder_out[0]
    ya = jnp.stack([enc[:, :256]] + [shift_y(enc[:, :256], k) for k in (1, 2, 3)])
    zb = jnp.stack([enc[:, 256:]] + [shift_z(enc[:, 256:], k) for k in (1, 2, 3)])
    pieces = [ya] + [shift_z(ya, k) for k in (1, 2, 3)]
    pieces += [zb] + [shift_y(zb, k) for k in (1, 2, 3)]

    qg = jnp.stack([queries[:, 0], grad_context[:, 0]], axis=1)
    two = jnp.stack([pick(qg, h), swap_yhi(pick(qg, 1 - h))])
    heads = jnp.stack([two[..., :256], two[..., 256:]])
    qg_own = pick(heads, c)
    qg_oth = swap_core(pick(heads, 1 - c))

    kv_send, kv_own = project(idx, pieces, w_key, w_value)
    kv_oth = swap_core(kv_send)
    gk, gv, gq = attend(kv_own, kv_oth, qg_own, qg_oth)

    e_keep, e_send = sort_pieces(idx, pieces)
    e_oth = swap_core(e_send)
    gk_o = swap_core(gk)
    gv_o = swap_core(gv)

    def rows_of(x, start):
        return lax.dynamic_slice_in_dim(x, start, 256, 0)

    away = (1 - h) * 256
    g_recv = swap_yhi(
        jnp.stack(
            [rows_of(gk, away), rows_of(gk_o, away + 512), rows_of(gv, away), rows_of(gv_o, away + 512)]
        )
    )

    def xor_lists(me):
        send = (jnp.stack([2 * (me ^ 1), 2 * (me ^ 2)]), jnp.stack([2 * (me ^ 3) + 1, 2 * (me ^ 2) + 1]))
        keep = (jnp.stack([2 * me, 2 * (me ^ 3)]), jnp.stack([2 * me + 1, 2 * (me ^ 1) + 1]))
        return [x.astype(jnp.int32) for x in send + keep]

    sa, sb, ka, kb = xor_lists(d)
    args = (e_keep, e_oth, gk, gk_o, gv, gv_o)
    send_a, send_b = weight_grads(idx, sa, sb, *args, BF)
    got_a, got_b = swap_x(send_a, 1), swap_x(send_b, 3)
    keep_a, keep_b = weight_grads(idx, ka, kb, *args, F32)
    part_a = keep_a + got_a.astype(F32)
    part_b = keep_b + got_b.astype(F32)
    last_a = swap_x(part_a[1].astype(BF), 3)
    last_b = swap_x(part_b[1].astype(BF), 1)
    done_a = (part_a[0] + last_a.astype(F32)).astype(BF)
    done_b = (part_b[0] + last_b.astype(F32)).astype(BF)
    mine = jnp.where(h == 0, done_a, done_b)
    theirs = swap_yhi(jnp.where(h == 0, done_b, done_a))
    grad_w = jnp.where(h == 0, jnp.stack([mine, theirs]), jnp.stack([theirs, mine]))

    sa, sb, ka, kb = xor_lists(z)
    args = (gk, gk_o, gv, gv_o, g_recv, w_key, w_value)
    send_a, send_b = encoder_grads(idx, sa, sb, *args, BF)
    got_a, got_b = swap_z(send_a, 1), swap_z(send_b, 3)
    keep_a, keep_b = encoder_grads(idx, ka, kb, *args, F32)
    part_a = keep_a + got_a.astype(F32)
    part_b = keep_b + got_b.astype(F32)
    last_a = swap_z(part_a[1].astype(BF), 3)
    last_b = swap_z(part_b[1].astype(BF), 1)
    done_a = part_a[0] + last_a.astype(F32)
    done_b = part_b[0] + last_b.astype(F32)
    mine = jnp.where(yl == 0, done_a, done_b)
    theirs = swap_ylo(jnp.where(yl == 0, done_b, done_a).astype(BF))
    grad_enc = (mine + theirs.astype(F32)).astype(BF)[None]

    gq = gq.reshape(2, 2, 128, 256)
    back = swap_core(gq[1])
    both = jnp.where(
        c == 0, jnp.concatenate([gq[0], back], axis=-1), jnp.concatenate([back, gq[0]], axis=-1)
    )
    theirs = swap_yhi(both[1])
    grad_q = jnp.where(h == 0, jnp.stack([both[0], theirs]), jnp.stack([theirs, both[0]]))[:, None]

    return grad_q, grad_enc, grad_w[..., :512], grad_w[..., 512:]


def solution(mesh):
    placed = (
        P("dp", "seq", "tensor"),
        P(None, None, "tensor"),
        P(None, None, "tensor"),
        P(None, "dp", "seq", "tensor"),
        P(None, "dp", "seq", "tensor"),
    )
    return jax.shard_map(
        on_device,
        mesh=mesh,
        in_specs=placed,
        out_specs=(
            P(None, "dp", "seq", "tensor"),
            P("dp", "seq", "tensor"),
            P(None, ("dp", "seq"), "tensor"),
            P(None, ("dp", "seq"), "tensor"),
        ),
        check_vma=False,
    )
```

```python
import jax
import jax.numpy as jnp
from jax import lax
from jax.experimental import pallas as pl
from jax.experimental.pallas import tpu as pltpu
from jax.sharding import PartitionSpec as P

DH = 256
BF = jnp.bfloat16
F32 = jnp.float32
NT = (((1,), (1,)), ((), ()))
TN = (((0,), (0,)), ((), ()))
MB = 1024 * 1024
VMEM = pl.BlockSpec(memory_space=pltpu.VMEM)
ANY = pl.BlockSpec(memory_space=pl.ANY)
H, C, Z, YL, D, T = range(6)


def arr(shape, dtype=BF):
    return jax.ShapeDtypeStruct(shape, dtype)


def call(body, name, inputs, outputs, scratch=(), hbm=(), mb=12, alias=None, flops=1):
    def wrapped(*refs):
        n = len(inputs)
        seq, t = lax.axis_index("seq"), lax.axis_index("tensor")
        place = [seq >> 1, seq & 1, t >> 1, t & 1, lax.axis_index("dp"), t]
        body(place, *refs[1:n], *refs[n + 1 :])

    args = [inputs[0]]
    specs = [ANY]
    for i, x in enumerate(inputs[1:]):
        pinned = i in hbm
        args.append(pltpu.with_memory_space_constraint(x, pltpu.HBM) if pinned else x)
        specs.append(ANY if pinned else VMEM)
    return pl.pallas_call(
        wrapped,
        in_specs=specs,
        out_specs=[ANY] + [VMEM] * len(outputs),
        out_shape=[arr(inputs[0].shape, inputs[0].dtype)] + list(outputs),
        scratch_shapes=list(scratch),
        input_output_aliases={0: 0, **(alias or {})},
        compiler_params=pltpu.CompilerParams(vmem_limit_bytes=mb * MB),
        cost_estimate=pl.CostEstimate(flops=flops, bytes_accessed=1, transcendentals=0),
        name=name,
    )(*args)


def swap_seq(x, m):
    return lax.ppermute(x, "seq", [(s, s ^ m) for s in range(4)])


def swap_ylo(x):
    return lax.ppermute(x, "tensor", [(t, t ^ 1) for t in range(8)])


def swap_x(x, m):
    return lax.ppermute(x, "dp", [(d, d ^ m) for d in range(4)])


def swap_z(x, m):
    return lax.ppermute(x, "tensor", [(t, t ^ (2 * m)) for t in range(8)])


def swap_y(x, m):
    pairs = []
    for s in range(4):
        for t in range(8):
            y = ((s // 2) * 2 + t % 2) ^ m
            pairs.append((s * 8 + t, ((y // 2) * 2 + s % 2) * 8 + (t // 2) * 2 + y % 2))
    return lax.ppermute(x, ("seq", "tensor"), pairs)


def cols(which):
    return pl.ds(pl.multiple_of(which * 256, 256), 256)


def join_body(idx, y0, y1, y2, y3, z0, z1, z2, z3, q, gc, ya, zb, qg_own, qg_send, sems):
    h = idx[H]
    copies = []
    for i, (layer, out) in enumerate(((h, qg_own), (1 - h, qg_send))):
        for n, x in enumerate((q, gc)):
            copies.append(pltpu.make_async_copy(x.at[layer, 0], out.at[n], sems.at[i, n]))
    for copy in copies:
        copy.start()
    ya[0, :256] = y0[...]
    ya[0, 256:] = y2[...]
    ya[1, :256] = y1[...]
    ya[1, 256:] = y3[...]
    zb[0] = z0[...]
    zb[1] = z1[...]
    zb[2] = z2[...]
    zb[3] = z3[...]
    for copy in copies:
        copy.wait()


def weight_rows(w, idx, m, b, which):
    base = (idx[Z] ^ m) * 1024 + (idx[YL] ^ b) * 512 + which * 256
    return w[idx[H], pl.ds(pl.multiple_of(base, 256), 256)]


def product(idx, w, terms):
    left = jnp.concatenate([block for block, _, _, _ in terms], axis=1)
    right = jnp.concatenate([weight_rows(w, idx, m, b, which) for _, m, b, which in terms], axis=0)
    return jnp.dot(left, right, preferred_element_type=F32)


def project_first_body(idx, wk, wv, ya, zb, az1, az3, by1, by3, acc, es):
    c = idx[C]
    terms = [(ya[0], 0, 0, c), (ya[1], 0, 1, c)]
    terms += [(az1[0], 1, 0, c), (az1[1], 1, 1, c), (az3[0], 3, 0, c), (az3[1], 3, 1, c)]
    terms += [(jnp.concatenate([by1[m], by3[m]], axis=0), m, 1, 1 - c) for m in range(4)]
    for n, w in enumerate((wk, wv)):
        at = slice(n * 512, n * 512 + 512)
        acc[:, at] = product(idx, w, terms)
        acc[:256, at] += product(idx, w, [(zb[m], m, 0, 1 - c) for m in range(4)])
    for n, b in enumerate((zb, by1, by3)):
        es[n] = b[...]


def project_last_body(idx, wk, wv, acc, az20, az21, by20, by21, send, keep, es, total):
    c = idx[C]
    by2 = [by20[0], by20[1], by21[0], by21[1]]
    for n, w in enumerate((wk, wv)):
        at = slice(n * 512, n * 512 + 512)
        total[:, at] = acc[:, at] + product(idx, w, [(az20[0], 2, 0, c), (az21[0], 2, 1, c)])
        total[256:, at] += product(idx, w, [(by2[m], m, 0, 1 - c) for m in range(4)])
    for out, which in ((keep, c), (send, 1 - c)):
        out[:, :256] = total[:, cols(which)].astype(BF)
        out[:, 256:] = total[:, cols(2 + which)].astype(BF)
    es[:2] = by20[...]
    es[2:] = by21[...]


def turn_keep_body(idx, ya, az1, az20, az21, az3, qg1, qg3, es_in, late_in, out, es, late):
    for r, block in enumerate(
        (ya[0], ya[1], az1[0], az1[1], az20[0], az21[0], az3[0], az3[1])
    ):
        out[r] = block.T


def turn_other_body(idx, es, late, out):
    for m in range(4):
        out[2 * m, :, :256] = es[0, m].T
        out[2 * m, :, 256:] = late[m].T
        out[2 * m + 1, :, :256] = es[1, m].T
        out[2 * m + 1, :, 256:] = es[2, m].T


def attend_body(idx, kv_own, kv_oth, qg0, qg1, qg2, qg3, g, g_far, gq_own, gq_core, gq_yhi, acc):
    mine = cols(idx[C])
    scale = DH ** (-0.5)
    acc[...] = jnp.zeros_like(acc)
    blocks = ((qg0, gq_own), (qg1, gq_core.at[0]), (qg2, gq_yhi), (qg3, gq_core.at[1]))
    for qg, gq in blocks:
        q = qg[0, :, mine]
        gc = qg[1, :, mine]
        s = [
            lax.dot_general(kv[:, :256], q, NT, preferred_element_type=F32) * scale
            for kv in (kv_own, kv_oth)
        ]
        top = jnp.maximum(
            jnp.max(s[0], axis=0, keepdims=True), jnp.max(s[1], axis=0, keepdims=True)
        )
        p = [jnp.exp(part - top) for part in s]
        total = jnp.sum(p[0], axis=0, keepdims=True) + jnp.sum(p[1], axis=0, keepdims=True)
        p = [part / total for part in p]
        dp = [
            lax.dot_general(kv[:, 256:], gc, NT, preferred_element_type=F32)
            for kv in (kv_own, kv_oth)
        ]
        delta = jnp.sum(p[0] * dp[0], axis=0, keepdims=True) + jnp.sum(
            p[1] * dp[1], axis=0, keepdims=True
        )
        ds = [(a * (b - delta) * scale).astype(BF) for a, b in zip(p, dp)]
        low = [a.astype(BF) for a in p]
        total_q = jnp.zeros((128, 256), F32)
        for part, kv in enumerate((kv_own, kv_oth)):
            rows = slice(part * 512, part * 512 + 512)
            acc[0, rows] += jnp.dot(ds[part], q, preferred_element_type=F32).astype(BF).astype(F32)
            acc[1, rows] += jnp.dot(low[part], gc, preferred_element_type=F32).astype(BF).astype(F32)
            total_q += lax.dot_general(ds[part], kv[:, :256], TN, preferred_element_type=F32)
        gq[...] = total_q.astype(BF)
    for n in range(2):
        g[n] = acc[n].astype(BF)
        g_far[0, n] = acc[n, 256:512].astype(BF)
        g_far[1, n] = acc[n, 768:].astype(BF)


def weight_job(idx, keep_t, oth_t, g, gp, n, dp_to, parity, out):
    r = (2 * dp_to + parity) ^ idx[T]
    own, oth = keep_t[r], oth_t[r]
    c = idx[C]
    left = jnp.dot(own, g[n, :512], preferred_element_type=F32)
    left += jnp.dot(oth, g[n, 512:], preferred_element_type=F32)
    right = jnp.dot(own, gp[n, 512:], preferred_element_type=F32)
    right += jnp.dot(oth, gp[n, :512], preferred_element_type=F32)
    out[:, cols(c)] = left.astype(out.dtype)
    out[:, cols(1 - c)] = right.astype(out.dtype)


SENT = ((1, 2), (3, 2))
KEPT = ((0, 3), (0, 1))


def weights_first_body(idx, keep_t, oth_t, g, gp, sk, sv):
    for n, out in enumerate((sk, sv)):
        for slot in range(2):
            weight_job(idx, keep_t, oth_t, g, gp, n, idx[D] ^ SENT[n][slot], 1 - idx[H], out.at[slot])


def weights_rest_body(idx, keep_t, oth_t, g, gp, sk, sv, k1k, k1v, k2k, k2v):
    for n, out in enumerate((sk, sv)):
        for slot in range(2):
            weight_job(idx, keep_t, oth_t, g, gp, n, idx[D] ^ SENT[n][slot], idx[H], out.at[slot])
    for parity, outs in ((1 - idx[H], (k1k, k1v)), (idx[H], (k2k, k2v))):
        for n, out in enumerate(outs):
            for slot in range(2):
                weight_job(idx, keep_t, oth_t, g, gp, n, idx[D] ^ KEPT[n][slot], parity, out.at[slot])


def add(keep, got, x, f):
    x[...] = (keep[1] + got[1].astype(F32)).astype(BF)
    f[...] = keep[0] + got[0].astype(F32)


def add_body(idx, ka, kb, ga, gb, xa, xb, fa, fb):
    add(ka, ga, xa, fa)
    add(kb, gb, xb, fb)


def pair_body(idx, fk, fv, gk, gv, sk_in, sv_in, gq0, gq1, gq2, pair, sk, sv, grad_q):
    pair[0] = (fk[...] + gk[...].astype(F32)).astype(BF)
    pair[1] = (fv[...] + gv[...].astype(F32)).astype(BF)
    h, c = idx[H], idx[C]
    grad_q[h, 0, :, cols(c)] = gq0[...]
    grad_q[h, 0, :, cols(1 - c)] = gq1[0]
    grad_q[1 - h, 0] = gq2[...]


def finish_weights_body(idx, fk, fv, gk, gv, theirs, wk, wv):
    h = idx[H]
    wk[h] = (fk[...] + gk[...].astype(F32)).astype(BF)
    wv[h] = (fv[...] + gv[...].astype(F32)).astype(BF)
    wk[1 - h] = theirs[0]
    wv[1 - h] = theirs[1]


def encoder_rows(idx, steps, parity, slot):
    start = ((idx[Z] ^ steps[parity][slot]) * 2 + parity) * 512
    return pl.ds(pl.multiple_of(start, 512), 512)


def turn_grads(idx, rhs, at, first, second):
    for n in range(2):
        rhs[cols(at + 2 * n + idx[C])] = first(n).T
        rhs[cols(at + 2 * n + 1 - idx[C])] = second(n).T


def encoder_own_body(idx, wk, wv, g, gp, out, rhs):
    turn_grads(idx, rhs, 0, lambda n: g[n, :256], lambda n: gp[n, 512:768])
    for slot in range(2):
        for parity in range(2):
            rows = encoder_rows(idx, SENT, parity, slot)
            left = jnp.concatenate([wk[idx[H], rows], wv[idx[H], rows]], axis=1)
            out[parity, slot] = jnp.dot(left, rhs[...], preferred_element_type=F32)


def relay_body(idx, x, out):
    pass


def encoder_sent_body(idx, wk, wv, own, far, far_core, gq_yhi, gq_got, out_a, out_b, gq_send, rhs):
    gq_send[:, cols(idx[C])] = gq_yhi[...]
    gq_send[:, cols(1 - idx[C])] = gq_got[1]
    turn_grads(idx, rhs, 0, lambda n: far[0, n], lambda n: far_core[0, n])
    for slot in range(2):
        for parity, out in enumerate((out_a, out_b)):
            rows = encoder_rows(idx, SENT, parity, slot)
            left = jnp.concatenate([wk[1 - idx[H], rows], wv[1 - idx[H], rows]], axis=1)
            total = own[parity, slot] + jnp.dot(left, rhs[...], preferred_element_type=F32)
            out[slot] = total.astype(BF)


def encoder_kept_body(idx, wk, wv, g, gp, far, far_core, out_a, out_b, rhs):
    turn_grads(idx, rhs, 0, lambda n: g[n, :256], lambda n: gp[n, 512:768])
    turn_grads(idx, rhs, 4, lambda n: far[0, n], lambda n: far_core[0, n])
    h = idx[H]
    for slot in range(2):
        for parity, out in enumerate((out_a, out_b)):
            rows = encoder_rows(idx, KEPT, parity, slot)
            left = jnp.concatenate([wk[h, rows], wv[h, rows], wk[1 - h, rows], wv[1 - h, rows]], axis=1)
            out[slot] = jnp.dot(left, rhs[...], preferred_element_type=F32)


def encoder_pair_body(idx, fa, fb, ga, gb, mine, theirs):
    yl = idx[YL]

    @pl.when(yl == 0)
    def _():
        mine[...] = fa[...] + ga[...].astype(F32)
        theirs[...] = (fb[...] + gb[...].astype(F32)).astype(BF)

    @pl.when(yl == 1)
    def _():
        mine[...] = fb[...] + gb[...].astype(F32)
        theirs[...] = (fa[...] + ga[...].astype(F32)).astype(BF)


def finish_encoder_body(idx, mine, theirs, out):
    out[0] = (mine[...] + theirs[...].astype(F32)).T.astype(BF)


def on_device(encoder_out, w_key, w_value, queries, grad_context):
    idx = jnp.zeros((8, 128), jnp.int32)
    c = lax.axis_index("seq") & 1
    dma = pltpu.SemaphoreType.DMA
    qg_block = arr((2, 128, 512))

    halves = jnp.stack([encoder_out[0, :, :256], encoder_out[0, :, 256:]])
    mine = lax.dynamic_index_in_dim(halves, c, 0, keepdims=False)
    other = lax.dynamic_index_in_dim(halves, 1 - c, 0, keepdims=False)
    parts = [mine] + [swap_y(mine, m) for m in (1, 2, 3)] + [other] + [swap_z(other, m) for m in (1, 2, 3)]
    idx, ya, zb, qg0, qg_send = call(
        join_body, "join", [idx, *parts, queries, grad_context],
        [arr((2, 512, 256)), arr((4, 256, 256)), qg_block, qg_block], [dma((2, 2))], hbm=(8, 9), flops=30_000_000_000,
    )
    az1, az3 = swap_z(ya, 1), swap_z(ya, 3)
    by1, by3 = swap_y(zb, 1), swap_y(zb, 3)
    az20, az21 = swap_z(az1[:1], 3), swap_z(az3[1:], 1)
    by20, by21 = swap_y(by1[:2], 3), swap_y(by3[2:], 1)

    ws = [w_key, w_value]
    qg2 = swap_seq(qg_send, 2)
    qg1, qg3 = swap_seq(qg0, 1), swap_seq(qg2, 1)
    idx, acc, es = call(
        project_first_body, "project_first", [idx, *ws, ya, zb, az1, az3, by1, by3],
        [arr((512, 1024), F32), arr((3, 4, 256, 256))],
    )
    idx, kv_send, kv_own, late = call(
        project_last_body, "project_last", [idx, *ws, acc, az20, az21, by20, by21],
        [arr((512, 512)), arr((512, 512)), arr((4, 256, 256))], [pltpu.VMEM((512, 1024), F32)],
    )
    kv_oth = swap_seq(kv_send, 1)
    idx, keep_t, es, late = call(
        turn_keep_body, "turn_keep", [idx, ya, az1, az20, az21, az3, qg1, qg3, es, late],
        [arr((8, 256, 512)), arr((3, 4, 256, 256)), arr((4, 256, 256))], alias={8: 2, 9: 3},
    )
    es_oth, late_oth = swap_seq(es, 1), swap_seq(late, 1)

    idx, g, g_far, gq_own, gq_core, gq_yhi = call(
        attend_body, "attend", [idx, kv_own, kv_oth, qg0, qg1, qg2, qg3],
        [arr((2, 1024, 256)), arr((2, 2, 256, 256)), arr((128, 256)), arr((2, 128, 256)), arr((128, 256))],
        [pltpu.VMEM((2, 1024, 256), F32)],
    )
    gp = swap_seq(g, 1)
    far = swap_seq(g_far, 2)
    gq_got = swap_seq(gq_core, 1)
    idx, oth_t = call(turn_other_body, "turn_other", [idx, es_oth, late_oth], [arr((8, 256, 512))])

    one, two = (256, 512), (2, 256, 512)
    mats = [keep_t, oth_t, g, gp]
    idx, s1k, s1v = call(weights_first_body, "weights_first", [idx, *mats], [arr(two)] * 2)
    got1k, got1v = swap_x(s1k, 1), swap_x(s1v, 3)
    idx, s2k, s2v, k1k, k1v, k2k, k2v = call(
        weights_rest_body, "weights_rest", [idx, *mats], [arr(two)] * 2 + [arr(two, F32)] * 4
    )

    one_t, two_t = (512, 256), (2, 512, 256)
    rhs = [pltpu.VMEM((2048, 256), BF)]
    rhs_half = [pltpu.VMEM((1024, 256), BF)]
    idx, own = call(
        encoder_own_body, "encoder_own", [idx, *ws, g, gp], [arr((2, *two_t), F32)], rhs_half
    )
    idx, far = call(relay_body, "relay", [idx, far], [arr((2, 2, 256, 256))], alias={1: 1})
    far_core = swap_seq(far[1:], 1)
    idx, ea, eb, gq_send = call(
        encoder_sent_body, "encoder_sent", [idx, *ws, own, far, far_core, gq_yhi, gq_got],
        [arr(two_t)] * 2 + [arr((128, 512))], rhs_half,
    )
    gq_theirs = swap_seq(gq_send, 2)
    got_a, got_b = swap_z(ea, 1), swap_z(eb, 3)
    idx, x1k, x1v, f1k, f1v = call(
        add_body, "add_first", [idx, k1k, k1v, got1k, got1v], [arr(one)] * 2 + [arr(one, F32)] * 2
    )
    last1k, last1v = swap_x(x1k, 3), swap_x(x1v, 1)
    idx, ka, kb = call(
        encoder_kept_body, "encoder_kept", [idx, *ws, g, gp, far, far_core], [arr(two_t, F32)] * 2, rhs
    )
    idx, pair, s2k, s2v, grad_q = call(
        pair_body, "weights_pair",
        [idx, f1k, f1v, last1k, last1v, s2k, s2v, gq_own, gq_got, gq_theirs],
        [arr(two)] * 3 + [arr((2, 1, 128, 512))], alias={5: 2, 6: 3},
    )
    w_theirs = swap_seq(pair, 2)
    got2k, got2v = swap_x(s2k, 1), swap_x(s2v, 3)
    idx, xa, xb, fa, fb = call(
        add_body, "encoder_add", [idx, ka, kb, got_a, got_b], [arr(one_t)] * 2 + [arr(one_t, F32)] * 2
    )
    last_a, last_b = swap_z(xa, 3), swap_z(xb, 1)
    idx, x2k, x2v, f2k, f2v = call(
        add_body, "weights_add", [idx, k2k, k2v, got2k, got2v], [arr(one)] * 2 + [arr(one, F32)] * 2
    )
    last2k, last2v = swap_x(x2k, 3), swap_x(x2v, 1)
    idx, e_mine, e_theirs = call(
        encoder_pair_body, "encoder_pair", [idx, fa, fb, last_a, last_b], [arr(one_t, F32), arr(one_t)]
    )
    e_got = swap_ylo(e_theirs)
    idx, grad_enc = call(finish_encoder_body, "finish_encoder", [idx, e_mine, e_got], [arr((1, 256, 512))])
    idx, grad_wk, grad_wv = call(
        finish_weights_body, "finish_weights", [idx, f2k, f2v, last2k, last2v, w_theirs], [arr(two)] * 2
    )
    return grad_q, grad_enc, grad_wk, grad_wv


def solution(mesh):
    placed = (
        P("dp", "seq", "tensor"),
        P(None, None, "tensor"),
        P(None, None, "tensor"),
        P(None, "dp", "seq", "tensor"),
        P(None, "dp", "seq", "tensor"),
    )
    return jax.shard_map(
        on_device,
        mesh=mesh,
        in_specs=placed,
        out_specs=(
            P(None, "dp", "seq", "tensor"),
            P("dp", "seq", "tensor"),
            P(None, ("dp", "seq"), "tensor"),
            P(None, ("dp", "seq"), "tensor"),
        ),
        check_vma=False,
    )
```

```python
import jax
import jax.numpy as jnp
from jax import lax
from jax.experimental import pallas as pl
from jax.experimental.pallas import tpu as pltpu
from jax.sharding import PartitionSpec as P

DH = 256
BF = jnp.bfloat16
F32 = jnp.float32
NT = (((1,), (1,)), ((), ()))
TN = (((0,), (0,)), ((), ()))
MB = 1024 * 1024
VMEM = pl.BlockSpec(memory_space=pltpu.VMEM)
ANY = pl.BlockSpec(memory_space=pl.ANY)
H, C, Z, YL, D, T = range(6)


def arr(shape, dtype=BF):
    return jax.ShapeDtypeStruct(shape, dtype)


def call(body, name, inputs, outputs, scratch=(), hbm=(), mb=12, alias=None, flops=1):
    def wrapped(*refs):
        n = len(inputs)
        seq, t = lax.axis_index("seq"), lax.axis_index("tensor")
        place = [seq >> 1, seq & 1, t >> 1, t & 1, lax.axis_index("dp"), t]
        body(place, *refs[1:n], *refs[n + 1 :])

    args = [inputs[0]]
    specs = [ANY]
    for i, x in enumerate(inputs[1:]):
        pinned = i in hbm
        args.append(pltpu.with_memory_space_constraint(x, pltpu.HBM) if pinned else x)
        specs.append(ANY if pinned else VMEM)
    return pl.pallas_call(
        wrapped,
        in_specs=specs,
        out_specs=[ANY] + [VMEM] * len(outputs),
        out_shape=[arr(inputs[0].shape, inputs[0].dtype)] + list(outputs),
        scratch_shapes=list(scratch),
        input_output_aliases={0: 0, **(alias or {})},
        compiler_params=pltpu.CompilerParams(vmem_limit_bytes=mb * MB),
        cost_estimate=pl.CostEstimate(flops=flops, bytes_accessed=1, transcendentals=0),
        name=name,
    )(*args)


def swap_seq(x, m):
    return lax.ppermute(x, "seq", [(s, s ^ m) for s in range(4)])


def swap_ylo(x):
    return lax.ppermute(x, "tensor", [(t, t ^ 1) for t in range(8)])


def swap_x(x, m):
    return lax.ppermute(x, "dp", [(d, d ^ m) for d in range(4)])


def swap_z(x, m):
    return lax.ppermute(x, "tensor", [(t, t ^ (2 * m)) for t in range(8)])


def swap_y(x, m):
    pairs = []
    for s in range(4):
        for t in range(8):
            y = ((s // 2) * 2 + t % 2) ^ m
            pairs.append((s * 8 + t, ((y // 2) * 2 + s % 2) * 8 + (t // 2) * 2 + y % 2))
    return lax.ppermute(x, ("seq", "tensor"), pairs)


def cols(which):
    return pl.ds(pl.multiple_of(which * 256, 256), 256)


def join_y_body(idx, y0, y1, y2, y3, q, gc, ya, qg_own, qg_send, sems):
    h = idx[H]
    copies = []
    for i, (layer, out) in enumerate(((h, qg_own), (1 - h, qg_send))):
        for n, x in enumerate((q, gc)):
            copies.append(pltpu.make_async_copy(x.at[layer, 0], out.at[n], sems.at[i, n]))
    for copy in copies:
        copy.start()
    ya[0, :256] = y0[...]
    ya[0, 256:] = y2[...]
    ya[1, :256] = y1[...]
    ya[1, 256:] = y3[...]
    for copy in copies:
        copy.wait()


def join_z_body(idx, z0, z1, z2, z3, zb):
    for m, z in enumerate((z0, z1, z2, z3)):
        zb[m] = z[...]


def weight_rows(w, idx, m, b, which):
    base = (idx[Z] ^ m) * 1024 + (idx[YL] ^ b) * 512 + which * 256
    return w[idx[H], pl.ds(pl.multiple_of(base, 256), 256)]


def product(idx, w, terms):
    left = jnp.concatenate([block for block, _, _, _ in terms], axis=1)
    right = jnp.concatenate([weight_rows(w, idx, m, b, which) for _, m, b, which in terms], axis=0)
    return jnp.dot(left, right, preferred_element_type=F32)


def project_first_body(idx, wk, wv, ya, zb, by1, by3, acc, es):
    c = idx[C]
    terms = [(ya[0], 0, 0, c), (ya[1], 0, 1, c)]
    terms += [(jnp.concatenate([by1[m], by3[m]], axis=0), m, 1, 1 - c) for m in range(4)]
    for n, w in enumerate((wk, wv)):
        at = slice(n * 512, n * 512 + 512)
        acc[:, at] = product(idx, w, terms)
        acc[:256, at] += product(idx, w, [(zb[m], m, 0, 1 - c) for m in range(4)])
    for m, b in ((0, zb), (1, by1), (3, by3)):
        es[4 * m : 4 * m + 4] = b[...]


def project_next_body(idx, wk, wv, acc_in, az1, az3, acc):
    c = idx[C]
    terms = [(az1[0], 1, 0, c), (az1[1], 1, 1, c), (az3[0], 3, 0, c), (az3[1], 3, 1, c)]
    for n, w in enumerate((wk, wv)):
        at = slice(n * 512, n * 512 + 512)
        acc[:, at] = acc_in[:, at] + product(idx, w, terms)


def project_last_body(idx, wk, wv, acc, by20, by21, az20, az21, qg_own, qg_far, es_in, send, keep, es, total):
    c = idx[C]
    by2 = [by20[0], by20[1], by21[0], by21[1]]
    for n, w in enumerate((wk, wv)):
        at = slice(n * 512, n * 512 + 512)
        total[:, at] = acc[:, at] + product(idx, w, [(az20[0], 2, 0, c), (az21[0], 2, 1, c)])
        total[256:, at] += product(idx, w, [(by2[m], m, 0, 1 - c) for m in range(4)])
    for out, which in ((keep, c), (send, 1 - c)):
        out[:512, :256] = total[:, cols(which)].astype(BF)
        out[:512, 256:] = total[:, cols(2 + which)].astype(BF)
    for i, qg in enumerate((qg_own, qg_far)):
        for n in range(2):
            send[512 + 128 * i : 640 + 128 * i, 256 * n : 256 * n + 256] = qg[n, :, cols(1 - c)]
    es[8:10] = by20[...]
    es[10:12] = by21[...]


def turn_keep_body(idx, ya, az1, az20, az21, az3, out):
    for r, block in enumerate(
        (ya[0], ya[1], az1[0], az1[1], az20[0], az21[0], az3[0], az3[1])
    ):
        out[r] = block.T


def turn_other_body(idx, es, out):
    for m in range(4):
        for b in range(2):
            out[2 * m + b, :, :256] = es[4 * b + m].T
            out[2 * m + b, :, 256:] = es[4 * (2 + b) + m].T


def attend_body(idx, kv_own, kv_oth, qg_own, qg_far, g, g_far, gq_own, gq_far, acc):
    mine = cols(idx[C])
    scale = DH ** (-0.5)
    acc[...] = jnp.zeros_like(acc)
    blocks = [
        (qg_own[0, :, mine], qg_own[1, :, mine], gq_own),
        (kv_oth[512:640, :256], kv_oth[512:640, 256:], g.at[2048:2176]),
        (qg_far[0, :, mine], qg_far[1, :, mine], gq_far),
        (kv_oth[640:, :256], kv_oth[640:, 256:], g.at[2176:]),
    ]
    for q, gc, gq in blocks:
        s = [
            lax.dot_general(kv[:512, :256], q, NT, preferred_element_type=F32) * scale
            for kv in (kv_own, kv_oth)
        ]
        top = jnp.maximum(
            jnp.max(s[0], axis=0, keepdims=True), jnp.max(s[1], axis=0, keepdims=True)
        )
        p = [jnp.exp(part - top) for part in s]
        total = jnp.sum(p[0], axis=0, keepdims=True) + jnp.sum(p[1], axis=0, keepdims=True)
        inverse = 1.0 / total
        p = [part * inverse for part in p]
        dp = [
            lax.dot_general(kv[:512, 256:], gc, NT, preferred_element_type=F32)
            for kv in (kv_own, kv_oth)
        ]
        delta = jnp.sum(p[0] * dp[0], axis=0, keepdims=True) + jnp.sum(
            p[1] * dp[1], axis=0, keepdims=True
        )
        ds = [(a * (b - delta) * scale).astype(BF) for a, b in zip(p, dp)]
        low = [a.astype(BF) for a in p]
        total_q = jnp.zeros((128, 256), F32)
        for part, kv in enumerate((kv_own, kv_oth)):
            rows = slice(part * 512, part * 512 + 512)
            acc[0, rows] += jnp.dot(ds[part], q, preferred_element_type=F32).astype(BF).astype(F32)
            acc[1, rows] += jnp.dot(low[part], gc, preferred_element_type=F32).astype(BF).astype(F32)
            total_q += lax.dot_general(ds[part], kv[:512, :256], TN, preferred_element_type=F32)
        gq[...] = total_q.astype(BF)
    for n in range(2):
        g[n * 1024 : n * 1024 + 1024] = acc[n].astype(BF)
        g_far[0, n * 256 : n * 256 + 256] = acc[n, 256:512].astype(BF)
        g_far[1, n * 256 : n * 256 + 256] = acc[n, 768:].astype(BF)


def weight_job(idx, keep_t, oth_t, g, gp, n, dp_to, parity, out):
    r = (2 * dp_to + parity) ^ idx[T]
    own, oth = keep_t[r], oth_t[r]
    c = idx[C]
    one, two = slice(n * 1024, n * 1024 + 512), slice(n * 1024 + 512, n * 1024 + 1024)
    left = jnp.dot(own, g[one], preferred_element_type=F32)
    left += jnp.dot(oth, g[two], preferred_element_type=F32)
    right = jnp.dot(own, gp[two], preferred_element_type=F32)
    right += jnp.dot(oth, gp[one], preferred_element_type=F32)
    out[:, cols(c)] = left.astype(out.dtype)
    out[:, cols(1 - c)] = right.astype(out.dtype)


SENT = ((1, 2), (3, 2))
KEPT = ((0, 3), (0, 1))


def weights_first_body(idx, keep_t, oth_t, g, gp, sk, sv):
    for n, out in enumerate((sk, sv)):
        for slot in range(2):
            weight_job(idx, keep_t, oth_t, g, gp, n, idx[D] ^ SENT[n][slot], 1 - idx[H], out.at[slot])


def weights_rest_body(idx, keep_t, oth_t, g, gp, sk, sv, k1k, k1v, k2k, k2v):
    for n, out in enumerate((sk, sv)):
        for slot in range(2):
            weight_job(idx, keep_t, oth_t, g, gp, n, idx[D] ^ SENT[n][slot], idx[H], out.at[slot])
    for parity, outs in ((1 - idx[H], (k1k, k1v)), (idx[H], (k2k, k2v))):
        for n, out in enumerate(outs):
            for slot in range(2):
                weight_job(idx, keep_t, oth_t, g, gp, n, idx[D] ^ KEPT[n][slot], parity, out.at[slot])


def add(keep, got, x, f):
    x[...] = (keep[1] + got[1].astype(F32)).astype(BF)
    f[...] = keep[0] + got[0].astype(F32)


def add_body(idx, ka, kb, ga, gb, xa, xb, fa, fb):
    add(ka, ga, xa, fa)
    add(kb, gb, xb, fb)


def add_body(idx, ka, kb, ga, gb, xa, xb, fa, fb):
    add(ka, ga, xa, fa)
    add(kb, gb, xb, fb)


def pair_body(idx, fk, fv, gk, gv, gq_far, gp, sk_in, sv_in, pair, sk, sv):
    pair[:256] = (fk[...] + gk[...].astype(F32)).astype(BF)
    pair[256:512] = (fv[...] + gv[...].astype(F32)).astype(BF)
    pair[512:, cols(idx[C])] = gq_far[...]
    pair[512:, cols(1 - idx[C])] = gp[2176:]


def finish_weights_body(idx, fk, fv, gk, gv, theirs, gq_own, gp, wk, wv, grad_q):
    h, c = idx[H], idx[C]
    wk[h] = (fk[...] + gk[...].astype(F32)).astype(BF)
    wv[h] = (fv[...] + gv[...].astype(F32)).astype(BF)
    wk[1 - h] = theirs[:256]
    wv[1 - h] = theirs[256:512]
    grad_q[h, 0, :, cols(c)] = gq_own[...]
    grad_q[h, 0, :, cols(1 - c)] = gp[2048:2176]
    grad_q[1 - h, 0] = theirs[512:]


def encoder_rows(idx, steps, parity, slot):
    start = ((idx[Z] ^ steps[parity][slot]) * 2 + parity) * 512
    return pl.ds(pl.multiple_of(start, 512), 512)


def turn_grads(idx, rhs, at, first, second):
    for n in range(2):
        rhs[cols(at + 2 * n + idx[C])] = first(n).T
        rhs[cols(at + 2 * n + 1 - idx[C])] = second(n).T


def encoder_own_body(idx, wk, wv, g, gp, out, rhs):
    turn_grads(idx, rhs, 0, lambda n: g[n * 1024 : n * 1024 + 256], lambda n: gp[n * 1024 + 512 : n * 1024 + 768])
    for slot in range(2):
        for parity in range(2):
            rows = encoder_rows(idx, SENT, parity, slot)
            left = jnp.concatenate([wk[idx[H], rows], wv[idx[H], rows]], axis=1)
            out[parity, slot] = jnp.dot(left, rhs[...], preferred_element_type=F32)


def relay_body(idx, *refs):
    pass


def encoder_sent_body(idx, wk, wv, own, far, far_core, out_a, out_b, rhs):
    turn_grads(idx, rhs, 0, lambda n: far[0, n * 256 : n * 256 + 256], lambda n: far_core[0, n * 256 : n * 256 + 256])
    for slot in range(2):
        for parity, out in enumerate((out_a, out_b)):
            rows = encoder_rows(idx, SENT, parity, slot)
            left = jnp.concatenate([wk[1 - idx[H], rows], wv[1 - idx[H], rows]], axis=1)
            total = own[parity, slot] + jnp.dot(left, rhs[...], preferred_element_type=F32)
            out[slot] = total.astype(BF)


def encoder_kept_body(idx, wk, wv, g, gp, far, far_core, out_a, out_b, rhs):
    turn_grads(idx, rhs, 0, lambda n: g[n * 1024 : n * 1024 + 256], lambda n: gp[n * 1024 + 512 : n * 1024 + 768])
    turn_grads(idx, rhs, 4, lambda n: far[0, n * 256 : n * 256 + 256], lambda n: far_core[0, n * 256 : n * 256 + 256])
    h = idx[H]
    for slot in range(2):
        for parity, out in enumerate((out_a, out_b)):
            rows = encoder_rows(idx, KEPT, parity, slot)
            left = jnp.concatenate([wk[h, rows], wv[h, rows], wk[1 - h, rows], wv[1 - h, rows]], axis=1)
            out[slot] = jnp.dot(left, rhs[...], preferred_element_type=F32)


def encoder_pair_body(idx, fa, fb, ga, gb, arrived, mine, theirs):
    yl = idx[YL]

    @pl.when(yl == 0)
    def _():
        mine[...] = fa[...] + ga[...].astype(F32)
        theirs[...] = (fb[...] + gb[...].astype(F32)).astype(BF)

    @pl.when(yl == 1)
    def _():
        mine[...] = fb[...] + gb[...].astype(F32)
        theirs[...] = (fa[...] + ga[...].astype(F32)).astype(BF)


def finish_encoder_body(idx, mine, theirs, out):
    out[0] = (mine[...] + theirs[...].astype(F32)).T.astype(BF)


def on_device(encoder_out, w_key, w_value, queries, grad_context):
    idx = jnp.zeros((8, 128), jnp.int32)
    c = lax.axis_index("seq") & 1
    dma = pltpu.SemaphoreType.DMA
    qg_block = arr((2, 128, 512))

    halves = jnp.stack([encoder_out[0, :, :256], encoder_out[0, :, 256:]])
    mine = lax.dynamic_index_in_dim(halves, c, 0, keepdims=False)
    other = lax.dynamic_index_in_dim(halves, 1 - c, 0, keepdims=False)
    from_y = [mine] + [swap_y(mine, m) for m in (1, 2, 3)]
    from_z = [other] + [swap_z(other, m) for m in (1, 2, 3)]
    idx, ya, qg0, qg_send = call(
        join_y_body, "join_y", [idx, *from_y, queries, grad_context],
        [arr((2, 512, 256)), qg_block, qg_block], [dma((2, 2))], hbm=(4, 5),
    )
    idx, zb = call(join_z_body, "join_z", [idx, *from_z], [arr((4, 256, 256))], flops=30_000_000_000)
    by1, by3 = swap_y(zb, 1), swap_y(zb, 3)
    az1, az3 = swap_z(ya, 1), swap_z(ya, 3)
    by20, by21 = swap_y(by1[:2], 3), swap_y(by3[2:], 1)
    az20, az21 = swap_z(az1[:1], 3), swap_z(az3[1:], 1)

    ws = [w_key, w_value]
    qg2 = swap_seq(qg_send, 2)
    idx, acc, es = call(
        project_first_body, "project_first", [idx, *ws, ya, zb, by1, by3],
        [arr((512, 1024), F32), arr((16, 256, 256))],
    )
    idx, acc = call(
        project_next_body, "project_next", [idx, *ws, acc, az1, az3], [arr((512, 1024), F32)]
    )
    idx, kv_send, kv_own, es = call(
        project_last_body, "project_last", [idx, *ws, acc, by20, by21, az20, az21, qg0, qg2, es],
        [arr((768, 512)), arr((512, 512)), arr((16, 256, 256))], [pltpu.VMEM((512, 1024), F32)],
        alias={10: 3},
    )
    kv_oth = swap_seq(kv_send, 1)
    idx, keep_t = call(
        turn_keep_body, "turn_keep", [idx, ya, az1, az20, az21, az3], [arr((8, 256, 512))]
    )
    idx, es = call(relay_body, "relay_rows", [idx, es, kv_oth], [arr((16, 256, 256))], alias={1: 1})
    es_oth = swap_seq(es, 1)

    idx, g, g_far, gq_own, gq_far = call(
        attend_body, "attend", [idx, kv_own, kv_oth, qg0, qg2],
        [arr((2304, 256)), arr((2, 512, 256)), arr((128, 256)), arr((128, 256))],
        [pltpu.VMEM((2, 1024, 256), F32)],
    )
    gp = swap_seq(g, 1)
    far = swap_seq(g_far, 2)
    idx, oth_t = call(turn_other_body, "turn_other", [idx, es_oth], [arr((8, 256, 512))])

    one, two = (256, 512), (2, 256, 512)
    mats = [keep_t, oth_t, g, gp]
    idx, s1k, s1v = call(weights_first_body, "weights_first", [idx, *mats], [arr(two)] * 2)
    got1k, got1v = swap_x(s1k, 1), swap_x(s1v, 3)
    idx, s2k, s2v, k1k, k1v, k2k, k2v = call(
        weights_rest_body, "weights_rest", [idx, *mats], [arr(two)] * 2 + [arr(two, F32)] * 4
    )

    one_t, two_t = (512, 256), (2, 512, 256)
    rhs = [pltpu.VMEM((2048, 256), BF)]
    rhs_half = [pltpu.VMEM((1024, 256), BF)]
    idx, own = call(
        encoder_own_body, "encoder_own", [idx, *ws, g, gp], [arr((2, *two_t), F32)], rhs_half
    )
    idx, far = call(relay_body, "relay", [idx, far], [arr((2, 512, 256))], alias={1: 1})
    far_core = swap_seq(far[1:], 1)
    idx, ea, eb = call(
        encoder_sent_body, "encoder_sent", [idx, *ws, own, far, far_core], [arr(two_t)] * 2, rhs_half
    )
    got_a, got_b = swap_z(ea, 1), swap_z(eb, 3)
    idx, x1k, x1v, f1k, f1v = call(
        add_body, "add_first", [idx, k1k, k1v, got1k, got1v], [arr(one)] * 2 + [arr(one, F32)] * 2
    )
    last1k, last1v = swap_x(x1k, 3), swap_x(x1v, 1)
    idx, ka, kb = call(
        encoder_kept_body, "encoder_kept",
        [idx, *ws, g, gp, far, far_core], [arr(two_t, F32)] * 2, rhs,
    )
    idx, pair, s2k, s2v = call(
        pair_body, "weights_pair", [idx, f1k, f1v, last1k, last1v, gq_far, gp, s2k, s2v],
        [arr((640, 512)), arr(two), arr(two)], alias={7: 2, 8: 3},
    )
    w_theirs = swap_seq(pair, 2)
    got2k, got2v = swap_x(s2k, 1), swap_x(s2v, 3)
    idx, xa, xb, fa, fb = call(
        add_body, "encoder_add", [idx, ka, kb, got_a, got_b], [arr(one_t)] * 2 + [arr(one_t, F32)] * 2
    )
    last_a, last_b = swap_z(xa, 3), swap_z(xb, 1)
    idx, x2k, x2v, f2k, f2v = call(
        add_body, "weights_add", [idx, k2k, k2v, got2k, got2v], [arr(one)] * 2 + [arr(one, F32)] * 2
    )
    last2k, last2v = swap_x(x2k, 3), swap_x(x2v, 1)
    idx, e_mine, e_theirs = call(
        encoder_pair_body, "encoder_pair", [idx, fa, fb, last_a, last_b, w_theirs], [arr(one_t, F32), arr(one_t)]
    )
    e_got = swap_ylo(e_theirs)
    idx, grad_wk, grad_wv, grad_q = call(
        finish_weights_body, "finish_weights",
        [idx, f2k, f2v, last2k, last2v, w_theirs, gq_own, gp],
        [arr(two)] * 2 + [arr((2, 1, 128, 512))],
    )
    idx, grad_enc = call(finish_encoder_body, "finish_encoder", [idx, e_mine, e_got], [arr((1, 256, 512))])
    return grad_q, grad_enc, grad_wk, grad_wv


def solution(mesh):
    placed = (
        P("dp", "seq", "tensor"),
        P(None, None, "tensor"),
        P(None, None, "tensor"),
        P(None, "dp", "seq", "tensor"),
        P(None, "dp", "seq", "tensor"),
    )
    return jax.shard_map(
        on_device,
        mesh=mesh,
        in_specs=placed,
        out_specs=(
            P(None, "dp", "seq", "tensor"),
            P("dp", "seq", "tensor"),
            P(None, ("dp", "seq"), "tensor"),
            P(None, ("dp", "seq"), "tensor"),
        ),
        check_vma=False,
    )
```

```python
import jax
import jax.numpy as jnp
from jax import lax
from jax.experimental import pallas as pl
from jax.experimental.pallas import tpu as pltpu
from jax.sharding import PartitionSpec as P

DH = 256
BF = jnp.bfloat16
F32 = jnp.float32
NT = (((1,), (1,)), ((), ()))
TN = (((0,), (0,)), ((), ()))
MB = 1024 * 1024
VMEM = pl.BlockSpec(memory_space=pltpu.VMEM)
ANY = pl.BlockSpec(memory_space=pl.ANY)
H, C, Z, YL, D, T = range(6)


def arr(shape, dtype=BF):
    return jax.ShapeDtypeStruct(shape, dtype)


def call(body, name, inputs, outputs, scratch=(), hbm=(), mb=12, alias=None, flops=1):
    def wrapped(*refs):
        n = len(inputs)
        seq, t = lax.axis_index("seq"), lax.axis_index("tensor")
        place = [seq >> 1, seq & 1, t >> 1, t & 1, lax.axis_index("dp"), t]
        body(place, *refs[1:n], *refs[n + 1 :])

    args = [inputs[0]]
    specs = [ANY]
    for i, x in enumerate(inputs[1:]):
        pinned = i in hbm
        args.append(pltpu.with_memory_space_constraint(x, pltpu.HBM) if pinned else x)
        specs.append(ANY if pinned else VMEM)
    return pl.pallas_call(
        wrapped,
        in_specs=specs,
        out_specs=[ANY] + [VMEM] * len(outputs),
        out_shape=[arr(inputs[0].shape, inputs[0].dtype)] + list(outputs),
        scratch_shapes=list(scratch),
        input_output_aliases={0: 0, **(alias or {})},
        compiler_params=pltpu.CompilerParams(vmem_limit_bytes=mb * MB),
        cost_estimate=pl.CostEstimate(flops=flops, bytes_accessed=1, transcendentals=0),
        name=name,
    )(*args)


def swap_seq(x, m):
    return lax.ppermute(x, "seq", [(s, s ^ m) for s in range(4)])


def swap_ylo(x):
    return lax.ppermute(x, "tensor", [(t, t ^ 1) for t in range(8)])


def swap_x(x, m):
    return lax.ppermute(x, "dp", [(d, d ^ m) for d in range(4)])


def swap_z(x, m):
    return lax.ppermute(x, "tensor", [(t, t ^ (2 * m)) for t in range(8)])


def swap_y(x, m):
    pairs = []
    for s in range(4):
        for t in range(8):
            y = ((s // 2) * 2 + t % 2) ^ m
            pairs.append((s * 8 + t, ((y // 2) * 2 + s % 2) * 8 + (t // 2) * 2 + y % 2))
    return lax.ppermute(x, ("seq", "tensor"), pairs)


def cols(which):
    return pl.ds(pl.multiple_of(which * 256, 256), 256)


def join_y_body(idx, y0, y1, y2, y3, q, gc, ya, qg_own, qg_send, sems):
    h = idx[H]
    copies = []
    for i, (layer, out) in enumerate(((h, qg_own), (1 - h, qg_send))):
        for n, x in enumerate((q, gc)):
            copies.append(pltpu.make_async_copy(x.at[layer, 0], out.at[n], sems.at[i, n]))
    for copy in copies:
        copy.start()
    ya[0, :256] = y0[...]
    ya[0, 256:] = y2[...]
    ya[1, :256] = y1[...]
    ya[1, 256:] = y3[...]
    for copy in copies:
        copy.wait()


def join_z_body(idx, z0, z1, z2, z3, zb):
    for m, z in enumerate((z0, z1, z2, z3)):
        zb[256 * m : 256 * m + 256] = z[...]
    zb[1024:] = jnp.zeros((32, 256), BF)


def weight_rows(w, idx, m, b, which):
    base = (idx[Z] ^ m) * 1024 + (idx[YL] ^ b) * 512 + which * 256
    return w[idx[H], pl.ds(pl.multiple_of(base, 256), 256)]


def product(idx, w, terms):
    left = jnp.concatenate([block for block, _, _, _ in terms], axis=1)
    right = jnp.concatenate([weight_rows(w, idx, m, b, which) for _, m, b, which in terms], axis=0)
    return jnp.dot(left, right, preferred_element_type=F32)


def block(x, m):
    return x[256 * m : 256 * m + 256]


def project_first_body(idx, wk, wv, ya, zb, by1, by3, acc, es):
    c = idx[C]
    terms = [(ya[0], 0, 0, c), (ya[1], 0, 1, c)]
    terms += [(jnp.concatenate([block(by1, m), block(by3, m)], axis=0), m, 1, 1 - c) for m in range(4)]
    for n, w in enumerate((wk, wv)):
        at = slice(n * 512, n * 512 + 512)
        acc[:, at] = product(idx, w, terms)
        acc[:256, at] += product(idx, w, [(block(zb, m), m, 0, 1 - c) for m in range(4)])
    for m, b in ((0, zb), (1, by1), (3, by3)):
        es[1024 * m : 1024 * m + 1024] = b[:1024]


def project_next_body(idx, wk, wv, acc_in, az1, az3, acc):
    c = idx[C]
    terms = [(az1[0], 1, 0, c), (az1[1], 1, 1, c), (az3[0], 3, 0, c), (az3[1], 3, 1, c)]
    for n, w in enumerate((wk, wv)):
        at = slice(n * 512, n * 512 + 512)
        acc[:, at] = acc_in[:, at] + product(idx, w, terms)


def project_last_body(idx, wk, wv, acc, by20, by21, az20, az21, qg_own, qg_far, es_in, send, keep, es, total):
    c = idx[C]
    by2 = [by20[:256], by20[256:512], by21[:256], by21[256:512]]
    for n, w in enumerate((wk, wv)):
        at = slice(n * 512, n * 512 + 512)
        total[:, at] = acc[:, at] + product(idx, w, [(az20[0], 2, 0, c), (az21[0], 2, 1, c)])
        total[256:, at] += product(idx, w, [(by2[m], m, 0, 1 - c) for m in range(4)])
    for out, which in ((keep, c), (send, 1 - c)):
        out[:512, :256] = total[:, cols(which)].astype(BF)
        out[:512, 256:] = total[:, cols(2 + which)].astype(BF)
    for i, qg in enumerate((qg_own, qg_far)):
        for n in range(2):
            send[512 + 128 * i : 640 + 128 * i, 256 * n : 256 * n + 256] = qg[n, :, cols(1 - c)]
    es[2048:2560] = by20[:512]
    es[2560:3072] = by21[:512]


def turn_keep_body(idx, ya, az1, az20, az21, az3, out):
    for r, block in enumerate(
        (ya[0], ya[1], az1[0], az1[1], az20[0], az21[0], az3[0], az3[1])
    ):
        out[r] = block.T


def turn_other_body(idx, es, out):
    for m in range(4):
        for b in range(2):
            out[2 * m + b, :, :256] = block(es, 4 * b + m).T
            out[2 * m + b, :, 256:] = block(es, 8 + 4 * b + m).T


def attend_body(idx, kv_own, kv_oth, qg_own, qg_far, g, g_far, gq_own, gq_far, acc):
    mine = cols(idx[C])
    scale = DH ** (-0.5)
    acc[...] = jnp.zeros_like(acc)
    blocks = [
        (qg_own[0, :, mine], qg_own[1, :, mine], gq_own),
        (kv_oth[512:640, :256], kv_oth[512:640, 256:], g.at[2048:2176]),
        (qg_far[0, :, mine], qg_far[1, :, mine], gq_far),
        (kv_oth[640:, :256], kv_oth[640:, 256:], g.at[2176:]),
    ]
    for q, gc, gq in blocks:
        s = [
            lax.dot_general(kv[:512, :256], q, NT, preferred_element_type=F32) * scale
            for kv in (kv_own, kv_oth)
        ]
        top = jnp.maximum(
            jnp.max(s[0], axis=0, keepdims=True), jnp.max(s[1], axis=0, keepdims=True)
        )
        p = [jnp.exp(part - top) for part in s]
        total = jnp.sum(p[0], axis=0, keepdims=True) + jnp.sum(p[1], axis=0, keepdims=True)
        inverse = 1.0 / total
        p = [part * inverse for part in p]
        dp = [
            lax.dot_general(kv[:512, 256:], gc, NT, preferred_element_type=F32)
            for kv in (kv_own, kv_oth)
        ]
        delta = jnp.sum(p[0] * dp[0], axis=0, keepdims=True) + jnp.sum(
            p[1] * dp[1], axis=0, keepdims=True
        )
        ds = [(a * (b - delta) * scale).astype(BF) for a, b in zip(p, dp)]
        low = [a.astype(BF) for a in p]
        total_q = jnp.zeros((128, 256), F32)
        for part, kv in enumerate((kv_own, kv_oth)):
            rows = slice(part * 512, part * 512 + 512)
            acc[0, rows] += jnp.dot(ds[part], q, preferred_element_type=F32).astype(BF).astype(F32)
            acc[1, rows] += jnp.dot(low[part], gc, preferred_element_type=F32).astype(BF).astype(F32)
            total_q += lax.dot_general(ds[part], kv[:512, :256], TN, preferred_element_type=F32)
        gq[...] = total_q.astype(BF)
    for n in range(2):
        g[n * 1024 : n * 1024 + 1024] = acc[n].astype(BF)
        g_far[0, n * 256 : n * 256 + 256] = acc[n, 256:512].astype(BF)
        g_far[1, n * 256 : n * 256 + 256] = acc[n, 768:].astype(BF)


def weight_job(idx, keep_t, oth_t, g, gp, n, dp_to, parity, out):
    r = (2 * dp_to + parity) ^ idx[T]
    own, oth = keep_t[r], oth_t[r]
    c = idx[C]
    one, two = slice(n * 1024, n * 1024 + 512), slice(n * 1024 + 512, n * 1024 + 1024)
    left = jnp.dot(own, g[one], preferred_element_type=F32)
    left += jnp.dot(oth, g[two], preferred_element_type=F32)
    right = jnp.dot(own, gp[two], preferred_element_type=F32)
    right += jnp.dot(oth, gp[one], preferred_element_type=F32)
    out[:, cols(c)] = left.astype(out.dtype)
    out[:, cols(1 - c)] = right.astype(out.dtype)


SENT = ((1, 2), (3, 2))
KEPT = ((0, 3), (0, 1))


def weights_first_body(idx, keep_t, oth_t, g, gp, sk, sv):
    for n, out in enumerate((sk, sv)):
        for slot in range(2):
            weight_job(idx, keep_t, oth_t, g, gp, n, idx[D] ^ SENT[n][slot], 1 - idx[H], out.at[slot])


def weights_rest_body(idx, keep_t, oth_t, g, gp, sk, sv, k1k, k1v, k2k, k2v):
    for n, out in enumerate((sk, sv)):
        for slot in range(2):
            weight_job(idx, keep_t, oth_t, g, gp, n, idx[D] ^ SENT[n][slot], idx[H], out.at[slot])
    for parity, outs in ((1 - idx[H], (k1k, k1v)), (idx[H], (k2k, k2v))):
        for n, out in enumerate(outs):
            for slot in range(2):
                weight_job(idx, keep_t, oth_t, g, gp, n, idx[D] ^ KEPT[n][slot], parity, out.at[slot])


def add(keep, got, x, f):
    x[...] = (keep[1] + got[1].astype(F32)).astype(BF)
    f[...] = keep[0] + got[0].astype(F32)


def add_body(idx, ka, kb, ga, gb, xa, xb, fa, fb):
    add(ka, ga, xa, fa)
    add(kb, gb, xb, fb)


def add_body(idx, ka, kb, ga, gb, xa, xb, fa, fb):
    add(ka, ga, xa, fa)
    add(kb, gb, xb, fb)


def pair_body(idx, fk, fv, gk, gv, gq_far, gp, sk_in, sv_in, pair, sk, sv):
    pair[:256] = (fk[...] + gk[...].astype(F32)).astype(BF)
    pair[256:512] = (fv[...] + gv[...].astype(F32)).astype(BF)
    pair[512:, cols(idx[C])] = gq_far[...]
    pair[512:, cols(1 - idx[C])] = gp[2176:]


def finish_weights_body(idx, fk, fv, gk, gv, theirs, gq_own, gp, wk, wv, grad_q):
    h, c = idx[H], idx[C]
    wk[h] = (fk[...] + gk[...].astype(F32)).astype(BF)
    wv[h] = (fv[...] + gv[...].astype(F32)).astype(BF)
    wk[1 - h] = theirs[:256]
    wv[1 - h] = theirs[256:512]
    grad_q[h, 0, :, cols(c)] = gq_own[...]
    grad_q[h, 0, :, cols(1 - c)] = gp[2048:2176]
    grad_q[1 - h, 0] = theirs[512:]


def encoder_rows(idx, steps, parity, slot):
    start = ((idx[Z] ^ steps[parity][slot]) * 2 + parity) * 512
    return pl.ds(pl.multiple_of(start, 512), 512)


def turn_grads(idx, rhs, at, first, second):
    for n in range(2):
        rhs[cols(at + 2 * n + idx[C])] = first(n).T
        rhs[cols(at + 2 * n + 1 - idx[C])] = second(n).T


def encoder_own_body(idx, wk, wv, g, gp, out, rhs):
    turn_grads(idx, rhs, 0, lambda n: g[n * 1024 : n * 1024 + 256], lambda n: gp[n * 1024 + 512 : n * 1024 + 768])
    for slot in range(2):
        for parity in range(2):
            rows = encoder_rows(idx, SENT, parity, slot)
            left = jnp.concatenate([wk[idx[H], rows], wv[idx[H], rows]], axis=1)
            out[parity, slot] = jnp.dot(left, rhs[...], preferred_element_type=F32)


def relay_body(idx, *refs):
    pass


def encoder_sent_body(idx, wk, wv, own, far, far_core, out_a, out_b, rhs):
    turn_grads(idx, rhs, 0, lambda n: far[0, n * 256 : n * 256 + 256], lambda n: far_core[0, n * 256 : n * 256 + 256])
    for slot in range(2):
        for parity, out in enumerate((out_a, out_b)):
            rows = encoder_rows(idx, SENT, parity, slot)
            left = jnp.concatenate([wk[1 - idx[H], rows], wv[1 - idx[H], rows]], axis=1)
            total = own[parity, slot] + jnp.dot(left, rhs[...], preferred_element_type=F32)
            out[slot] = total.astype(BF)


def encoder_kept_body(idx, wk, wv, g, gp, far, far_core, out_a, out_b, rhs):
    turn_grads(idx, rhs, 0, lambda n: g[n * 1024 : n * 1024 + 256], lambda n: gp[n * 1024 + 512 : n * 1024 + 768])
    turn_grads(idx, rhs, 4, lambda n: far[0, n * 256 : n * 256 + 256], lambda n: far_core[0, n * 256 : n * 256 + 256])
    h = idx[H]
    for slot in range(2):
        for parity, out in enumerate((out_a, out_b)):
            rows = encoder_rows(idx, KEPT, parity, slot)
            left = jnp.concatenate([wk[h, rows], wv[h, rows], wk[1 - h, rows], wv[1 - h, rows]], axis=1)
            out[slot] = jnp.dot(left, rhs[...], preferred_element_type=F32)


def encoder_pair_body(idx, fa, fb, ga, gb, arrived, mine, theirs):
    yl = idx[YL]

    @pl.when(yl == 0)
    def _():
        mine[...] = fa[...] + ga[...].astype(F32)
        theirs[...] = (fb[...] + gb[...].astype(F32)).astype(BF)

    @pl.when(yl == 1)
    def _():
        mine[...] = fb[...] + gb[...].astype(F32)
        theirs[...] = (fa[...] + ga[...].astype(F32)).astype(BF)


def finish_encoder_body(idx, mine, theirs, out):
    out[0] = (mine[...] + theirs[...].astype(F32)).T.astype(BF)


def on_device(encoder_out, w_key, w_value, queries, grad_context):
    idx = jnp.zeros((8, 128), jnp.int32)
    c = lax.axis_index("seq") & 1
    dma = pltpu.SemaphoreType.DMA
    qg_block = arr((2, 128, 512))

    halves = jnp.stack([encoder_out[0, :, :256], encoder_out[0, :, 256:]])
    mine = lax.dynamic_index_in_dim(halves, c, 0, keepdims=False)
    other = lax.dynamic_index_in_dim(halves, 1 - c, 0, keepdims=False)
    from_y = [mine] + [swap_y(mine, m) for m in (1, 2, 3)]
    from_z = [other] + [swap_z(other, m) for m in (1, 2, 3)]
    idx, zb = call(join_z_body, "join_z", [idx, *from_z], [arr((1056, 256))])
    idx, ya, qg0, qg_send = call(
        join_y_body, "join_y", [idx, *from_y, queries, grad_context],
        [arr((2, 512, 256)), qg_block, qg_block], [dma((2, 2))], hbm=(4, 5), flops=30_000_000_000,
    )
    by1, by3 = swap_y(zb, 1), swap_y(zb, 3)
    az1, az3 = swap_z(ya, 1), swap_z(ya, 3)
    by20, by21 = swap_y(by1[:528], 3), swap_y(by3[512:1040], 1)
    az20, az21 = swap_z(az1[:1], 3), swap_z(az3[1:], 1)

    ws = [w_key, w_value]
    qg2 = swap_seq(qg_send, 2)
    idx, acc, es = call(
        project_first_body, "project_first", [idx, *ws, ya, zb, by1, by3],
        [arr((512, 1024), F32), arr((4096, 256))],
    )
    idx, acc = call(
        project_next_body, "project_next", [idx, *ws, acc, az1, az3], [arr((512, 1024), F32)]
    )
    idx, kv_send, kv_own, es = call(
        project_last_body, "project_last", [idx, *ws, acc, by20, by21, az20, az21, qg0, qg2, es],
        [arr((768, 512)), arr((512, 512)), arr((4096, 256))], [pltpu.VMEM((512, 1024), F32)],
        alias={10: 3},
    )
    kv_oth = swap_seq(kv_send, 1)
    idx, keep_t = call(
        turn_keep_body, "turn_keep", [idx, ya, az1, az20, az21, az3], [arr((8, 256, 512))]
    )
    idx, es = call(relay_body, "relay_rows", [idx, es, kv_oth], [arr((4096, 256))], alias={1: 1})
    es_oth = swap_seq(es, 1)

    idx, g, g_far, gq_own, gq_far = call(
        attend_body, "attend", [idx, kv_own, kv_oth, qg0, qg2],
        [arr((2304, 256)), arr((2, 512, 256)), arr((128, 256)), arr((128, 256))],
        [pltpu.VMEM((2, 1024, 256), F32)],
    )
    gp = swap_seq(g, 1)
    far = swap_seq(g_far, 2)
    idx, oth_t = call(turn_other_body, "turn_other", [idx, es_oth], [arr((8, 256, 512))])

    one, two = (256, 512), (2, 256, 512)
    mats = [keep_t, oth_t, g, gp]
    idx, s1k, s1v = call(weights_first_body, "weights_first", [idx, *mats], [arr(two)] * 2)
    got1k, got1v = swap_x(s1k, 1), swap_x(s1v, 3)
    idx, s2k, s2v, k1k, k1v, k2k, k2v = call(
        weights_rest_body, "weights_rest", [idx, *mats], [arr(two)] * 2 + [arr(two, F32)] * 4
    )

    one_t, two_t = (512, 256), (2, 512, 256)
    rhs = [pltpu.VMEM((2048, 256), BF)]
    rhs_half = [pltpu.VMEM((1024, 256), BF)]
    idx, own = call(
        encoder_own_body, "encoder_own", [idx, *ws, g, gp], [arr((2, *two_t), F32)], rhs_half
    )
    idx, far = call(relay_body, "relay", [idx, far], [arr((2, 512, 256))], alias={1: 1})
    far_core = swap_seq(far[1:], 1)
    idx, ea, eb = call(
        encoder_sent_body, "encoder_sent", [idx, *ws, own, far, far_core], [arr(two_t)] * 2, rhs_half
    )
    got_a, got_b = swap_z(ea, 1), swap_z(eb, 3)
    idx, x1k, x1v, f1k, f1v = call(
        add_body, "add_first", [idx, k1k, k1v, got1k, got1v], [arr(one)] * 2 + [arr(one, F32)] * 2
    )
    last1k, last1v = swap_x(x1k, 3), swap_x(x1v, 1)
    idx, ka, kb = call(
        encoder_kept_body, "encoder_kept",
        [idx, *ws, g, gp, far, far_core], [arr(two_t, F32)] * 2, rhs,
    )
    idx, pair, s2k, s2v = call(
        pair_body, "weights_pair", [idx, f1k, f1v, last1k, last1v, gq_far, gp, s2k, s2v],
        [arr((640, 512)), arr(two), arr(two)], alias={7: 2, 8: 3},
    )
    w_theirs = swap_seq(pair, 2)
    got2k, got2v = swap_x(s2k, 1), swap_x(s2v, 3)
    idx, xa, xb, fa, fb = call(
        add_body, "encoder_add", [idx, ka, kb, got_a, got_b], [arr(one_t)] * 2 + [arr(one_t, F32)] * 2
    )
    last_a, last_b = swap_z(xa, 3), swap_z(xb, 1)
    idx, x2k, x2v, f2k, f2v = call(
        add_body, "weights_add", [idx, k2k, k2v, got2k, got2v], [arr(one)] * 2 + [arr(one, F32)] * 2
    )
    last2k, last2v = swap_x(x2k, 3), swap_x(x2v, 1)
    idx, e_mine, e_theirs = call(
        encoder_pair_body, "encoder_pair", [idx, fa, fb, last_a, last_b, w_theirs], [arr(one_t, F32), arr(one_t)]
    )
    e_got = swap_ylo(e_theirs)
    idx, grad_wk, grad_wv, grad_q = call(
        finish_weights_body, "finish_weights",
        [idx, f2k, f2v, last2k, last2v, w_theirs, gq_own, gp],
        [arr(two)] * 2 + [arr((2, 1, 128, 512))],
    )
    idx, grad_enc = call(finish_encoder_body, "finish_encoder", [idx, e_mine, e_got], [arr((1, 256, 512))])
    return grad_q, grad_enc, grad_wk, grad_wv


def solution(mesh):
    placed = (
        P("dp", "seq", "tensor"),
        P(None, None, "tensor"),
        P(None, None, "tensor"),
        P(None, "dp", "seq", "tensor"),
        P(None, "dp", "seq", "tensor"),
    )
    return jax.shard_map(
        on_device,
        mesh=mesh,
        in_specs=placed,
        out_specs=(
            P(None, "dp", "seq", "tensor"),
            P("dp", "seq", "tensor"),
            P(None, ("dp", "seq"), "tensor"),
            P(None, ("dp", "seq"), "tensor"),
        ),
        check_vma=False,
    )
```

```python
import jax
import jax.numpy as jnp
from jax import lax
from jax.experimental import pallas as pl
from jax.experimental.pallas import tpu as pltpu
from jax.sharding import PartitionSpec as P

DH = 256
BF = jnp.bfloat16
F32 = jnp.float32
NT = (((1,), (1,)), ((), ()))
TN = (((0,), (0,)), ((), ()))
MB = 1024 * 1024
VMEM = pl.BlockSpec(memory_space=pltpu.VMEM)
ANY = pl.BlockSpec(memory_space=pl.ANY)
H, C, Z, YL, D, T = range(6)


def arr(shape, dtype=BF):
    return jax.ShapeDtypeStruct(shape, dtype)


def call(body, name, inputs, outputs, scratch=(), hbm=(), mb=12, alias=None, flops=1):
    def wrapped(*refs):
        n = len(inputs)
        seq, t = lax.axis_index("seq"), lax.axis_index("tensor")
        place = [seq >> 1, seq & 1, t >> 1, t & 1, lax.axis_index("dp"), t]
        body(place, *refs[1:n], *refs[n + 1 :])

    args = [inputs[0]]
    specs = [ANY]
    for i, x in enumerate(inputs[1:]):
        pinned = i in hbm
        args.append(pltpu.with_memory_space_constraint(x, pltpu.HBM) if pinned else x)
        specs.append(ANY if pinned else VMEM)
    return pl.pallas_call(
        wrapped,
        in_specs=specs,
        out_specs=[ANY] + [VMEM] * len(outputs),
        out_shape=[arr(inputs[0].shape, inputs[0].dtype)] + list(outputs),
        scratch_shapes=list(scratch),
        input_output_aliases={0: 0, **(alias or {})},
        compiler_params=pltpu.CompilerParams(vmem_limit_bytes=mb * MB),
        cost_estimate=pl.CostEstimate(flops=flops, bytes_accessed=1, transcendentals=0),
        name=name,
    )(*args)


def swap_seq(x, m):
    return lax.ppermute(x, "seq", [(s, s ^ m) for s in range(4)])


def swap_ylo(x):
    return lax.ppermute(x, "tensor", [(t, t ^ 1) for t in range(8)])


def swap_x(x, m):
    return lax.ppermute(x, "dp", [(d, d ^ m) for d in range(4)])


def swap_z(x, m):
    return lax.ppermute(x, "tensor", [(t, t ^ (2 * m)) for t in range(8)])


def swap_y(x, m):
    pairs = []
    for s in range(4):
        for t in range(8):
            y = ((s // 2) * 2 + t % 2) ^ m
            pairs.append((s * 8 + t, ((y // 2) * 2 + s % 2) * 8 + (t // 2) * 2 + y % 2))
    return lax.ppermute(x, ("seq", "tensor"), pairs)


def cols(which):
    return pl.ds(pl.multiple_of(which * 256, 256), 256)


def join_y_body(idx, y0, y1, y2, y3, q, gc, ya, qg_own, qg_send, sems):
    h = idx[H]
    copies = []
    for i, (layer, out) in enumerate(((h, qg_own), (1 - h, qg_send))):
        for n, x in enumerate((q, gc)):
            copies.append(pltpu.make_async_copy(x.at[layer, 0], out.at[n], sems.at[i, n]))
    for copy in copies:
        copy.start()
    ya[0, :256] = y0[...]
    ya[0, 256:] = y2[...]
    ya[1, :256] = y1[...]
    ya[1, 256:] = y3[...]
    for copy in copies:
        copy.wait()


def join_z_body(idx, z0, z1, z2, z3, zb):
    for m, z in enumerate((z0, z1, z2, z3)):
        zb[256 * m : 256 * m + 256] = z[...]
    zb[1024:] = jnp.zeros((16, 256), BF)


def weight_at(idx, m, b, which):
    base = (idx[Z] ^ m) * 1024 + (idx[YL] ^ b) * 512 + which * 256
    return pl.ds(pl.multiple_of(base, 256), 256)


def weight_rows(w, idx, m, b, which):
    return w[idx[H], weight_at(idx, m, b, which)]


def product(idx, w, terms):
    left = jnp.concatenate([block for block, _, _, _ in terms], axis=1)
    right = jnp.concatenate([weight_rows(w, idx, m, b, which) for _, m, b, which in terms], axis=0)
    return jnp.dot(left, right, preferred_element_type=F32)


def block(x, m):
    return x[256 * m : 256 * m + 256]


def project_first_body(idx, wk, wv, ya, zb, by1, by3, acc, es):
    c = idx[C]
    terms = [(ya[0], 0, 0, c), (ya[1], 0, 1, c)]
    terms += [(jnp.concatenate([block(by1, m), block(by3, m)], axis=0), m, 1, 1 - c) for m in range(4)]
    for n, w in enumerate((wk, wv)):
        at = slice(n * 512, n * 512 + 512)
        acc[:, at] = product(idx, w, terms)
        acc[:256, at] += product(idx, w, [(block(zb, m), m, 0, 1 - c) for m in range(4)])
    for m, b in ((0, zb), (1, by1), (3, by3)):
        es[1024 * m : 1024 * m + 1024] = b[:1024]


def project_next_body(idx, wk, wv, acc_in, az1, az3, acc):
    c = idx[C]
    terms = [(az1[0], 1, 0, c), (az1[1], 1, 1, c), (az3[0], 3, 0, c), (az3[1], 3, 1, c)]
    for n, w in enumerate((wk, wv)):
        at = slice(n * 512, n * 512 + 512)
        acc[:, at] = acc_in[:, at] + product(idx, w, terms)


def project_last_body(idx, wk, wv, acc, by20, by21, az20, az21, qg_own, qg_far, send, keep):
    h, c = idx[H], idx[C]
    across = jnp.concatenate([az20[0], az21[0]], axis=1)
    late = jnp.concatenate([by20[:256], by20[256:512], by21[:256], by21[256:512]], axis=1)
    for out, head in ((send, 1 - c), (keep, c)):
        for n, w in enumerate((wk, wv)):
            rows = [weight_at(idx, 2, b, c) for b in range(2)]
            right = jnp.concatenate([w[h, at, cols(head)] for at in rows], axis=0)
            part = acc[:, cols(2 * n + head)] + jnp.dot(across, right, preferred_element_type=F32)
            rows = [weight_at(idx, m, 0, 1 - c) for m in range(4)]
            right = jnp.concatenate([w[h, at, cols(head)] for at in rows], axis=0)
            more = jnp.dot(late, right, preferred_element_type=F32)
            out[:256, 256 * n : 256 * n + 256] = part[:256].astype(BF)
            out[256:512, 256 * n : 256 * n + 256] = (part[256:] + more).astype(BF)
    for i, qg in enumerate((qg_own, qg_far)):
        for n in range(2):
            send[512 + 128 * i : 640 + 128 * i, 256 * n : 256 * n + 256] = qg[n, :, cols(1 - c)]


def turn_keep_body(idx, ya, az1, az20, az21, az3, by20, by21, es_in, out, es):
    es[2048:2560] = by20[:512]
    es[2560:3072] = by21[:512]
    for r, block in enumerate(
        (ya[0], ya[1], az1[0], az1[1], az20[0], az21[0], az3[0], az3[1])
    ):
        out[r] = block.T


def turn_other_body(idx, es, out):
    for m in range(4):
        for b in range(2):
            out[2 * m + b, :, :256] = block(es, 4 * b + m).T
            out[2 * m + b, :, 256:] = block(es, 8 + 4 * b + m).T


def attend_body(idx, kv_own, kv_oth, qg_own, qg_far, g, g_far, gq_own, gq_far, ds_all, low_all):
    mine = cols(idx[C])
    scale = DH ** (-0.5)
    blocks = [
        (qg_own[0, :, mine], qg_own[1, :, mine], gq_own),
        (kv_oth[512:640, :256], kv_oth[512:640, 256:], g.at[2048:2176]),
        (qg_far[0, :, mine], qg_far[1, :, mine], gq_far),
        (kv_oth[640:, :256], kv_oth[640:, 256:], g.at[2176:]),
    ]
    for n, (q, gc, _) in enumerate(blocks):
        at = slice(128 * n, 128 * n + 128)
        s = [
            lax.dot_general(kv[:512, :256], q, NT, preferred_element_type=F32) * scale
            for kv in (kv_own, kv_oth)
        ]
        top = jnp.maximum(
            jnp.max(s[0], axis=0, keepdims=True), jnp.max(s[1], axis=0, keepdims=True)
        )
        p = [jnp.exp(part - top) for part in s]
        total = jnp.sum(p[0], axis=0, keepdims=True) + jnp.sum(p[1], axis=0, keepdims=True)
        inverse = 1.0 / total
        p = [part * inverse for part in p]
        dp = [
            lax.dot_general(kv[:512, 256:], gc, NT, preferred_element_type=F32)
            for kv in (kv_own, kv_oth)
        ]
        delta = jnp.sum(p[0] * dp[0], axis=0, keepdims=True) + jnp.sum(
            p[1] * dp[1], axis=0, keepdims=True
        )
        for part in range(2):
            rows = slice(512 * part, 512 * part + 512)
            ds_all[rows, at] = (p[part] * (dp[part] - delta) * scale).astype(BF)
            low_all[rows, at] = p[part].astype(BF)
    keys_t = jnp.concatenate([kv_own[:, :256].T, kv_oth[:512, :256].T], axis=1)
    gq_t = jnp.dot(keys_t, ds_all[...], preferred_element_type=F32)
    for n, (_, _, out) in enumerate(blocks):
        out[...] = gq_t[:, 128 * n : 128 * n + 128].T.astype(BF)
    for chunk in range(4):
        rows = slice(256 * chunk, 256 * chunk + 256)
        for kind, source in enumerate((ds_all, low_all)):
            total = None
            for n, pair in enumerate(blocks):
                left = source[rows, 128 * n : 128 * n + 128]
                part = jnp.dot(left, pair[kind], preferred_element_type=F32).astype(BF).astype(F32)
                total = part if total is None else total + part
            low = total.astype(BF)
            g[1024 * kind + 256 * chunk : 1024 * kind + 256 * chunk + 256] = low
            if chunk % 2 == 1:
                g_far[chunk // 2, 256 * kind : 256 * kind + 256] = low


def weight_job(idx, keep_t, oth_t, g, gp, n, dp_to, parity, out):
    r = (2 * dp_to + parity) ^ idx[T]
    own, oth = keep_t[r], oth_t[r]
    c = idx[C]
    one, two = slice(n * 1024, n * 1024 + 512), slice(n * 1024 + 512, n * 1024 + 1024)
    left = jnp.dot(own, g[one], preferred_element_type=F32)
    left += jnp.dot(oth, g[two], preferred_element_type=F32)
    right = jnp.dot(own, gp[two], preferred_element_type=F32)
    right += jnp.dot(oth, gp[one], preferred_element_type=F32)
    out[:, cols(c)] = left.astype(out.dtype)
    out[:, cols(1 - c)] = right.astype(out.dtype)


SENT = ((1, 2), (3, 2))
KEPT = ((0, 3), (0, 1))


def weights_first_body(idx, keep_t, oth_t, g, gp, sk, sv):
    for n, out in enumerate((sk, sv)):
        for slot in range(2):
            weight_job(idx, keep_t, oth_t, g, gp, n, idx[D] ^ SENT[n][slot], 1 - idx[H], out.at[slot])


def weights_rest_body(idx, keep_t, oth_t, g, gp, sk, sv, k1k, k1v, k2k, k2v):
    for n, out in enumerate((sk, sv)):
        for slot in range(2):
            weight_job(idx, keep_t, oth_t, g, gp, n, idx[D] ^ SENT[n][slot], idx[H], out.at[slot])
    for parity, outs in ((1 - idx[H], (k1k, k1v)), (idx[H], (k2k, k2v))):
        for n, out in enumerate(outs):
            for slot in range(2):
                weight_job(idx, keep_t, oth_t, g, gp, n, idx[D] ^ KEPT[n][slot], parity, out.at[slot])


def add(keep, got, x, f):
    x[...] = (keep[1] + got[1].astype(F32)).astype(BF)
    f[...] = keep[0] + got[0].astype(F32)


def add_body(idx, ka, kb, ga, gb, xa, xb, fa, fb):
    add(ka, ga, xa, fa)
    add(kb, gb, xb, fb)


def add_body(idx, ka, kb, ga, gb, xa, xb, fa, fb):
    add(ka, ga, xa, fa)
    add(kb, gb, xb, fb)


def pair_body(idx, fk, fv, gk, gv, gq_far, gp, sk_in, sv_in, pair, sk, sv):
    pair[:256] = (fk[...] + gk[...].astype(F32)).astype(BF)
    pair[256:512] = (fv[...] + gv[...].astype(F32)).astype(BF)
    pair[512:, cols(idx[C])] = gq_far[...]
    pair[512:, cols(1 - idx[C])] = gp[2176:]


def finish_weights_body(idx, fk, fv, gk, gv, theirs, gq_own, gp, wk, wv, grad_q):
    h, c = idx[H], idx[C]
    wk[h] = (fk[...] + gk[...].astype(F32)).astype(BF)
    wv[h] = (fv[...] + gv[...].astype(F32)).astype(BF)
    wk[1 - h] = theirs[:256]
    wv[1 - h] = theirs[256:512]
    grad_q[h, 0, :, cols(c)] = gq_own[...]
    grad_q[h, 0, :, cols(1 - c)] = gp[2048:2176]
    grad_q[1 - h, 0] = theirs[512:]


def encoder_rows(idx, steps, parity, slot):
    start = ((idx[Z] ^ steps[parity][slot]) * 2 + parity) * 512
    return pl.ds(pl.multiple_of(start, 512), 512)


def turn_grads(idx, rhs, at, first, second):
    for n in range(2):
        rhs[cols(at + 2 * n + idx[C])] = first(n).T
        rhs[cols(at + 2 * n + 1 - idx[C])] = second(n).T


def encoder_own_body(idx, wk, wv, g, gp, out, rhs):
    turn_grads(idx, rhs, 0, lambda n: g[n * 1024 : n * 1024 + 256], lambda n: gp[n * 1024 + 512 : n * 1024 + 768])
    for slot in range(2):
        for parity in range(2):
            rows = encoder_rows(idx, SENT, parity, slot)
            left = jnp.concatenate([wk[idx[H], rows], wv[idx[H], rows]], axis=1)
            out[parity, slot] = jnp.dot(left, rhs[...], preferred_element_type=F32)


def relay_body(idx, *refs):
    pass


def encoder_sent_body(idx, wk, wv, own, far, far_core, out_a, out_b, rhs):
    turn_grads(idx, rhs, 0, lambda n: far[0, n * 256 : n * 256 + 256], lambda n: far_core[0, n * 256 : n * 256 + 256])
    for slot in range(2):
        for parity, out in enumerate((out_a, out_b)):
            rows = encoder_rows(idx, SENT, parity, slot)
            left = jnp.concatenate([wk[1 - idx[H], rows], wv[1 - idx[H], rows]], axis=1)
            total = own[parity, slot] + jnp.dot(left, rhs[...], preferred_element_type=F32)
            out[slot] = total.astype(BF)


def encoder_kept_body(idx, wk, wv, g, gp, far, far_core, out_a, out_b, rhs):
    turn_grads(idx, rhs, 0, lambda n: g[n * 1024 : n * 1024 + 256], lambda n: gp[n * 1024 + 512 : n * 1024 + 768])
    turn_grads(idx, rhs, 4, lambda n: far[0, n * 256 : n * 256 + 256], lambda n: far_core[0, n * 256 : n * 256 + 256])
    h = idx[H]
    for slot in range(2):
        for parity, out in enumerate((out_a, out_b)):
            rows = encoder_rows(idx, KEPT, parity, slot)
            left = jnp.concatenate([wk[h, rows], wv[h, rows], wk[1 - h, rows], wv[1 - h, rows]], axis=1)
            out[slot] = jnp.dot(left, rhs[...], preferred_element_type=F32)


def encoder_pair_body(idx, fa, fb, ga, gb, arrived, mine, theirs):
    yl = idx[YL]

    @pl.when(yl == 0)
    def _():
        mine[...] = fa[...] + ga[...].astype(F32)
        theirs[...] = (fb[...] + gb[...].astype(F32)).astype(BF)

    @pl.when(yl == 1)
    def _():
        mine[...] = fb[...] + gb[...].astype(F32)
        theirs[...] = (fa[...] + ga[...].astype(F32)).astype(BF)


def finish_encoder_body(idx, mine, theirs, out):
    out[0] = (mine[...] + theirs[...].astype(F32)).T.astype(BF)


def on_device(encoder_out, w_key, w_value, queries, grad_context):
    idx = jnp.zeros((8, 128), jnp.int32)
    c = lax.axis_index("seq") & 1
    dma = pltpu.SemaphoreType.DMA
    qg_block = arr((2, 128, 512))

    halves = jnp.stack([encoder_out[0, :, :256], encoder_out[0, :, 256:]])
    mine = lax.dynamic_index_in_dim(halves, c, 0, keepdims=False)
    other = lax.dynamic_index_in_dim(halves, 1 - c, 0, keepdims=False)
    from_y = [mine] + [swap_y(mine, m) for m in (1, 2, 3)]
    from_z = [other] + [swap_z(other, m) for m in (1, 2, 3)]
    idx, zb = call(join_z_body, "join_z", [idx, *from_z], [arr((1040, 256))])
    idx, ya, qg0, qg_send = call(
        join_y_body, "join_y", [idx, *from_y, queries, grad_context],
        [arr((2, 512, 256)), qg_block, qg_block], [dma((2, 2))], hbm=(4, 5), flops=30_000_000_000,
    )
    by1, by3 = swap_y(zb, 1), swap_y(zb, 3)
    az1, az3 = swap_z(ya, 1), swap_z(ya, 3)
    by20, by21 = swap_y(by1[:528], 3), swap_y(by3[512:1040], 1)
    az20, az21 = swap_z(az1[:1], 3), swap_z(az3[1:], 1)

    ws = [w_key, w_value]
    qg2 = swap_seq(qg_send, 2)
    idx, acc, es = call(
        project_first_body, "project_first", [idx, *ws, ya, zb, by1, by3],
        [arr((512, 1024), F32), arr((4096, 256))],
    )
    idx, acc = call(
        project_next_body, "project_next", [idx, *ws, acc, az1, az3], [arr((512, 1024), F32)]
    )
    idx, kv_send, kv_own = call(
        project_last_body, "project_last", [idx, *ws, acc, by20, by21, az20, az21, qg0, qg2],
        [arr((768, 512)), arr((512, 512))],
    )
    kv_oth = swap_seq(kv_send, 1)
    idx, keep_t, es = call(
        turn_keep_body, "turn_keep", [idx, ya, az1, az20, az21, az3, by20, by21, es],
        [arr((8, 256, 512)), arr((4096, 256))], alias={8: 2},
    )
    idx, es = call(relay_body, "relay_rows", [idx, es, kv_oth], [arr((4096, 256))], alias={1: 1})
    es_oth = swap_seq(es, 1)

    idx, g, g_far, gq_own, gq_far = call(
        attend_body, "attend", [idx, kv_own, kv_oth, qg0, qg2],
        [arr((2304, 256)), arr((2, 512, 256)), arr((128, 256)), arr((128, 256))],
        [pltpu.VMEM((1024, 512), BF)] * 2,
    )
    gp = swap_seq(g, 1)
    far = swap_seq(g_far, 2)
    idx, oth_t = call(turn_other_body, "turn_other", [idx, es_oth], [arr((8, 256, 512))])

    one, two = (256, 512), (2, 256, 512)
    mats = [keep_t, oth_t, g, gp]
    idx, s1k, s1v = call(weights_first_body, "weights_first", [idx, *mats], [arr(two)] * 2)
    got1k, got1v = swap_x(s1k, 1), swap_x(s1v, 3)
    idx, s2k, s2v, k1k, k1v, k2k, k2v = call(
        weights_rest_body, "weights_rest", [idx, *mats], [arr(two)] * 2 + [arr(two, F32)] * 4
    )

    one_t, two_t = (512, 256), (2, 512, 256)
    rhs = [pltpu.VMEM((2048, 256), BF)]
    rhs_half = [pltpu.VMEM((1024, 256), BF)]
    idx, own = call(
        encoder_own_body, "encoder_own", [idx, *ws, g, gp], [arr((2, *two_t), F32)], rhs_half
    )
    idx, far = call(relay_body, "relay", [idx, far], [arr((2, 512, 256))], alias={1: 1})
    far_core = swap_seq(far[1:], 1)
    idx, ea, eb = call(
        encoder_sent_body, "encoder_sent", [idx, *ws, own, far, far_core], [arr(two_t)] * 2, rhs_half
    )
    got_a, got_b = swap_z(ea, 1), swap_z(eb, 3)
    idx, x1k, x1v, f1k, f1v = call(
        add_body, "add_first", [idx, k1k, k1v, got1k, got1v], [arr(one)] * 2 + [arr(one, F32)] * 2
    )
    last1k, last1v = swap_x(x1k, 3), swap_x(x1v, 1)
    idx, ka, kb = call(
        encoder_kept_body, "encoder_kept",
        [idx, *ws, g, gp, far, far_core], [arr(two_t, F32)] * 2, rhs,
    )
    idx, pair, s2k, s2v = call(
        pair_body, "weights_pair", [idx, f1k, f1v, last1k, last1v, gq_far, gp, s2k, s2v],
        [arr((640, 512)), arr(two), arr(two)], alias={7: 2, 8: 3},
    )
    w_theirs = swap_seq(pair, 2)
    got2k, got2v = swap_x(s2k, 1), swap_x(s2v, 3)
    idx, xa, xb, fa, fb = call(
        add_body, "encoder_add", [idx, ka, kb, got_a, got_b], [arr(one_t)] * 2 + [arr(one_t, F32)] * 2
    )
    last_a, last_b = swap_z(xa, 3), swap_z(xb, 1)
    idx, x2k, x2v, f2k, f2v = call(
        add_body, "weights_add", [idx, k2k, k2v, got2k, got2v], [arr(one)] * 2 + [arr(one, F32)] * 2
    )
    last2k, last2v = swap_x(x2k, 3), swap_x(x2v, 1)
    idx, e_mine, e_theirs = call(
        encoder_pair_body, "encoder_pair", [idx, fa, fb, last_a, last_b, w_theirs], [arr(one_t, F32), arr(one_t)]
    )
    e_got = swap_ylo(e_theirs)
    idx, grad_wk, grad_wv, grad_q = call(
        finish_weights_body, "finish_weights",
        [idx, f2k, f2v, last2k, last2v, w_theirs, gq_own, gp],
        [arr(two)] * 2 + [arr((2, 1, 128, 512))],
    )
    idx, grad_enc = call(finish_encoder_body, "finish_encoder", [idx, e_mine, e_got], [arr((1, 256, 512))])
    return grad_q, grad_enc, grad_wk, grad_wv


def solution(mesh):
    placed = (
        P("dp", "seq", "tensor"),
        P(None, None, "tensor"),
        P(None, None, "tensor"),
        P(None, "dp", "seq", "tensor"),
        P(None, "dp", "seq", "tensor"),
    )
    return jax.shard_map(
        on_device,
        mesh=mesh,
        in_specs=placed,
        out_specs=(
            P(None, "dp", "seq", "tensor"),
            P("dp", "seq", "tensor"),
            P(None, ("dp", "seq"), "tensor"),
            P(None, ("dp", "seq"), "tensor"),
        ),
        check_vma=False,
    )
```

```python
import jax
import jax.numpy as jnp
from jax import lax
from jax.experimental import pallas as pl
from jax.experimental.pallas import tpu as pltpu
from jax.sharding import PartitionSpec as P

DH = 256
BF = jnp.bfloat16
F32 = jnp.float32
NT = (((1,), (1,)), ((), ()))
TN = (((0,), (0,)), ((), ()))
MB = 1024 * 1024
VMEM = pl.BlockSpec(memory_space=pltpu.VMEM)
ANY = pl.BlockSpec(memory_space=pl.ANY)
H, C, Z, YL, D, T = range(6)


def arr(shape, dtype=BF):
    return jax.ShapeDtypeStruct(shape, dtype)


def call(body, name, inputs, outputs, scratch=(), hbm=(), mb=12, alias=None, flops=1):
    def wrapped(*refs):
        n = len(inputs)
        seq, t = lax.axis_index("seq"), lax.axis_index("tensor")
        place = [seq >> 1, seq & 1, t >> 1, t & 1, lax.axis_index("dp"), t]
        body(place, *refs[1:n], *refs[n + 1 :])

    args = [inputs[0]]
    specs = [ANY]
    for i, x in enumerate(inputs[1:]):
        pinned = i in hbm
        args.append(pltpu.with_memory_space_constraint(x, pltpu.HBM) if pinned else x)
        specs.append(ANY if pinned else VMEM)
    return pl.pallas_call(
        wrapped,
        in_specs=specs,
        out_specs=[ANY] + [VMEM] * len(outputs),
        out_shape=[arr(inputs[0].shape, inputs[0].dtype)] + list(outputs),
        scratch_shapes=list(scratch),
        input_output_aliases={0: 0, **(alias or {})},
        compiler_params=pltpu.CompilerParams(vmem_limit_bytes=mb * MB),
        cost_estimate=pl.CostEstimate(flops=flops, bytes_accessed=1, transcendentals=0),
        name=name,
    )(*args)


def swap_seq(x, m):
    return lax.ppermute(x, "seq", [(s, s ^ m) for s in range(4)])


def swap_ylo(x):
    return lax.ppermute(x, "tensor", [(t, t ^ 1) for t in range(8)])


def swap_x(x, m):
    return lax.ppermute(x, "dp", [(d, d ^ m) for d in range(4)])


def swap_z(x, m):
    return lax.ppermute(x, "tensor", [(t, t ^ (2 * m)) for t in range(8)])


def swap_y(x, m):
    pairs = []
    for s in range(4):
        for t in range(8):
            y = ((s // 2) * 2 + t % 2) ^ m
            pairs.append((s * 8 + t, ((y // 2) * 2 + s % 2) * 8 + (t // 2) * 2 + y % 2))
    return lax.ppermute(x, ("seq", "tensor"), pairs)


def cols(which):
    return pl.ds(pl.multiple_of(which * 256, 256), 256)


def join_y_body(idx, y0, y1, y2, y3, q, gc, ya, qg_own, qg_send):
    ya[0, :256] = y0[...]
    ya[0, 256:] = y2[...]
    ya[1, :256] = y1[...]
    ya[1, 256:] = y3[...]
    for layer, out in ((idx[H], qg_own), (1 - idx[H], qg_send)):
        out[:128] = q[layer, 0]
        out[128:256] = gc[layer, 0]
        out[256:] = jnp.zeros((16, 512), BF)


def join_z_body(idx, z0, z1, z2, z3, zb):
    for m, z in enumerate((z0, z1, z2, z3)):
        zb[256 * m : 256 * m + 256] = z[...]
    zb[1024:] = jnp.zeros((16, 256), BF)


def weight_at(idx, m, b, which):
    base = (idx[Z] ^ m) * 1024 + (idx[YL] ^ b) * 512 + which * 256
    return pl.ds(pl.multiple_of(base, 256), 256)


def weight_rows(w, idx, m, b, which):
    return w[idx[H], weight_at(idx, m, b, which)]


def product(idx, w, terms):
    left = jnp.concatenate([block for block, _, _, _ in terms], axis=1)
    right = jnp.concatenate([weight_rows(w, idx, m, b, which) for _, m, b, which in terms], axis=0)
    return jnp.dot(left, right, preferred_element_type=F32)


def block(x, m):
    return x[256 * m : 256 * m + 256]


def project_first_body(idx, wk, wv, ya, zb, by1, by3, acc, es):
    c = idx[C]
    terms = [(ya[0], 0, 0, c), (ya[1], 0, 1, c)]
    terms += [(jnp.concatenate([block(by1, m), block(by3, m)], axis=0), m, 1, 1 - c) for m in range(4)]
    for n, w in enumerate((wk, wv)):
        at = slice(n * 512, n * 512 + 512)
        acc[:, at] = product(idx, w, terms)
        acc[:256, at] += product(idx, w, [(block(zb, m), m, 0, 1 - c) for m in range(4)])
    for m, b in ((0, zb), (1, by1), (3, by3)):
        es[1024 * m : 1024 * m + 1024] = b[:1024]


def project_next_body(idx, wk, wv, acc_in, az1, az3, acc):
    c = idx[C]
    terms = [(az1[0], 1, 0, c), (az1[1], 1, 1, c), (az3[0], 3, 0, c), (az3[1], 3, 1, c)]
    for n, w in enumerate((wk, wv)):
        at = slice(n * 512, n * 512 + 512)
        acc[:, at] = acc_in[:, at] + product(idx, w, terms)


def project_last_body(idx, wk, wv, acc, by20, by21, az20, az21, qg_own, qg_far, send, keep):
    h, c = idx[H], idx[C]
    across = jnp.concatenate([az20[0], az21[0]], axis=1)
    late = jnp.concatenate([by20[:256], by20[256:512], by21[:256], by21[256:512]], axis=1)
    for out, head in ((send, 1 - c), (keep, c)):
        for n, w in enumerate((wk, wv)):
            rows = [weight_at(idx, 2, b, c) for b in range(2)]
            right = jnp.concatenate([w[h, at, cols(head)] for at in rows], axis=0)
            part = acc[:, cols(2 * n + head)] + jnp.dot(across, right, preferred_element_type=F32)
            rows = [weight_at(idx, m, 0, 1 - c) for m in range(4)]
            right = jnp.concatenate([w[h, at, cols(head)] for at in rows], axis=0)
            more = jnp.dot(late, right, preferred_element_type=F32)
            out[:256, 256 * n : 256 * n + 256] = part[:256].astype(BF)
            out[256:512, 256 * n : 256 * n + 256] = (part[256:] + more).astype(BF)
    for i, qg in enumerate((qg_own, qg_far)):
        for n in range(2):
            send[512 + 128 * i : 640 + 128 * i, 256 * n : 256 * n + 256] = qg[128 * n : 128 * n + 128, cols(1 - c)]


def turn_keep_body(idx, ya, az1, az20, az21, az3, by20, by21, es_in, out, es):
    es[2048:2560] = by20[:512]
    es[2560:3072] = by21[:512]
    for r, block in enumerate(
        (ya[0], ya[1], az1[0], az1[1], az20[0], az21[0], az3[0], az3[1])
    ):
        out[r] = block.T


def turn_other_body(idx, es, out):
    for m in range(4):
        for b in range(2):
            out[2 * m + b, :, :256] = block(es, 4 * b + m).T
            out[2 * m + b, :, 256:] = block(es, 8 + 4 * b + m).T


def attend_body(idx, kv_own, kv_oth, qg_own, qg_far, g, g_far, gq_own, gq_far, ds_all, low_all):
    mine = cols(idx[C])
    scale = DH ** (-0.5)
    blocks = [
        (qg_own[:128, mine], qg_own[128:256, mine], gq_own),
        (kv_oth[512:640, :256], kv_oth[512:640, 256:], g.at[2048:2176]),
        (qg_far[:128, mine], qg_far[128:256, mine], gq_far),
        (kv_oth[640:, :256], kv_oth[640:, 256:], g.at[2176:]),
    ]
    for n, (q, gc, _) in enumerate(blocks):
        at = slice(128 * n, 128 * n + 128)
        s = [
            lax.dot_general(kv[:512, :256], q, NT, preferred_element_type=F32) * scale
            for kv in (kv_own, kv_oth)
        ]
        top = jnp.maximum(
            jnp.max(s[0], axis=0, keepdims=True), jnp.max(s[1], axis=0, keepdims=True)
        )
        p = [jnp.exp(part - top) for part in s]
        total = jnp.sum(p[0], axis=0, keepdims=True) + jnp.sum(p[1], axis=0, keepdims=True)
        inverse = 1.0 / total
        p = [part * inverse for part in p]
        dp = [
            lax.dot_general(kv[:512, 256:], gc, NT, preferred_element_type=F32)
            for kv in (kv_own, kv_oth)
        ]
        delta = jnp.sum(p[0] * dp[0], axis=0, keepdims=True) + jnp.sum(
            p[1] * dp[1], axis=0, keepdims=True
        )
        for part in range(2):
            rows = slice(512 * part, 512 * part + 512)
            ds_all[rows, at] = (p[part] * (dp[part] - delta) * scale).astype(BF)
            low_all[rows, at] = p[part].astype(BF)
    keys_t = jnp.concatenate([kv_own[:, :256].T, kv_oth[:512, :256].T], axis=1)
    gq_t = jnp.dot(keys_t, ds_all[...], preferred_element_type=F32)
    for n, (_, _, out) in enumerate(blocks):
        out[...] = gq_t[:, 128 * n : 128 * n + 128].T.astype(BF)
    for chunk in range(4):
        rows = slice(256 * chunk, 256 * chunk + 256)
        for kind, source in enumerate((ds_all, low_all)):
            total = None
            for n, pair in enumerate(blocks):
                left = source[rows, 128 * n : 128 * n + 128]
                part = jnp.dot(left, pair[kind], preferred_element_type=F32).astype(BF).astype(F32)
                total = part if total is None else total + part
            low = total.astype(BF)
            g[1024 * kind + 256 * chunk : 1024 * kind + 256 * chunk + 256] = low
            if chunk % 2 == 1:
                g_far[chunk // 2, 256 * kind : 256 * kind + 256] = low


def weight_job(idx, keep_t, oth_t, g, gp, n, dp_to, parity, out):
    r = (2 * dp_to + parity) ^ idx[T]
    own, oth = keep_t[r], oth_t[r]
    c = idx[C]
    one, two = slice(n * 1024, n * 1024 + 512), slice(n * 1024 + 512, n * 1024 + 1024)
    left = jnp.dot(own, g[one], preferred_element_type=F32)
    left += jnp.dot(oth, g[two], preferred_element_type=F32)
    right = jnp.dot(own, gp[two], preferred_element_type=F32)
    right += jnp.dot(oth, gp[one], preferred_element_type=F32)
    out[:, cols(c)] = left.astype(out.dtype)
    out[:, cols(1 - c)] = right.astype(out.dtype)


SENT = ((1, 2), (3, 2))
KEPT = ((0, 3), (0, 1))


def weights_first_body(idx, keep_t, oth_t, g, gp, sk, sv):
    for n, out in enumerate((sk, sv)):
        for slot in range(2):
            weight_job(idx, keep_t, oth_t, g, gp, n, idx[D] ^ SENT[n][slot], 1 - idx[H], out.at[slot])


def weights_rest_body(idx, keep_t, oth_t, g, gp, sk, sv, k1k, k1v, k2k, k2v):
    for n, out in enumerate((sk, sv)):
        for slot in range(2):
            weight_job(idx, keep_t, oth_t, g, gp, n, idx[D] ^ SENT[n][slot], idx[H], out.at[slot])
    for parity, outs in ((1 - idx[H], (k1k, k1v)), (idx[H], (k2k, k2v))):
        for n, out in enumerate(outs):
            for slot in range(2):
                weight_job(idx, keep_t, oth_t, g, gp, n, idx[D] ^ KEPT[n][slot], parity, out.at[slot])


def add(keep, got, x, f):
    x[...] = (keep[1] + got[1].astype(F32)).astype(BF)
    f[...] = keep[0] + got[0].astype(F32)


def add_body(idx, ka, kb, ga, gb, xa, xb, fa, fb):
    add(ka, ga, xa, fa)
    add(kb, gb, xb, fb)


def add_body(idx, ka, kb, ga, gb, xa, xb, fa, fb):
    add(ka, ga, xa, fa)
    add(kb, gb, xb, fb)


def pair_body(idx, fk, fv, gk, gv, gq_far, gp, sk_in, sv_in, pair, sk, sv):
    pair[:256] = (fk[...] + gk[...].astype(F32)).astype(BF)
    pair[256:512] = (fv[...] + gv[...].astype(F32)).astype(BF)
    pair[512:, cols(idx[C])] = gq_far[...]
    pair[512:, cols(1 - idx[C])] = gp[2176:]


def finish_weights_body(idx, fk, fv, gk, gv, theirs, gq_own, gp, wk, wv, grad_q):
    h, c = idx[H], idx[C]
    wk[h] = (fk[...] + gk[...].astype(F32)).astype(BF)
    wv[h] = (fv[...] + gv[...].astype(F32)).astype(BF)
    wk[1 - h] = theirs[:256]
    wv[1 - h] = theirs[256:512]
    grad_q[h, 0, :, cols(c)] = gq_own[...]
    grad_q[h, 0, :, cols(1 - c)] = gp[2048:2176]
    grad_q[1 - h, 0] = theirs[512:]


def encoder_rows(idx, steps, parity, slot):
    start = ((idx[Z] ^ steps[parity][slot]) * 2 + parity) * 512
    return pl.ds(pl.multiple_of(start, 512), 512)


def turn_grads(idx, rhs, at, first, second):
    for n in range(2):
        rhs[cols(at + 2 * n + idx[C])] = first(n).T
        rhs[cols(at + 2 * n + 1 - idx[C])] = second(n).T


def encoder_own_body(idx, wk, wv, g, gp, out, rhs):
    turn_grads(idx, rhs, 0, lambda n: g[n * 1024 : n * 1024 + 256], lambda n: gp[n * 1024 + 512 : n * 1024 + 768])
    for slot in range(2):
        for parity in range(2):
            rows = encoder_rows(idx, SENT, parity, slot)
            left = jnp.concatenate([wk[idx[H], rows], wv[idx[H], rows]], axis=1)
            out[parity, slot] = jnp.dot(left, rhs[...], preferred_element_type=F32)


def relay_body(idx, *refs):
    pass


def encoder_sent_body(idx, wk, wv, own, far, far_core, out_a, out_b, rhs):
    turn_grads(idx, rhs, 0, lambda n: far[0, n * 256 : n * 256 + 256], lambda n: far_core[0, n * 256 : n * 256 + 256])
    for slot in range(2):
        for parity, out in enumerate((out_a, out_b)):
            rows = encoder_rows(idx, SENT, parity, slot)
            left = jnp.concatenate([wk[1 - idx[H], rows], wv[1 - idx[H], rows]], axis=1)
            total = own[parity, slot] + jnp.dot(left, rhs[...], preferred_element_type=F32)
            out[slot] = total.astype(BF)


def encoder_kept_body(idx, wk, wv, g, gp, far, far_core, out_a, out_b, rhs):
    turn_grads(idx, rhs, 0, lambda n: g[n * 1024 : n * 1024 + 256], lambda n: gp[n * 1024 + 512 : n * 1024 + 768])
    turn_grads(idx, rhs, 4, lambda n: far[0, n * 256 : n * 256 + 256], lambda n: far_core[0, n * 256 : n * 256 + 256])
    h = idx[H]
    for slot in range(2):
        for parity, out in enumerate((out_a, out_b)):
            rows = encoder_rows(idx, KEPT, parity, slot)
            left = jnp.concatenate([wk[h, rows], wv[h, rows], wk[1 - h, rows], wv[1 - h, rows]], axis=1)
            out[slot] = jnp.dot(left, rhs[...], preferred_element_type=F32)


def encoder_pair_body(idx, fa, fb, ga, gb, arrived, mine, theirs):
    yl = idx[YL]

    @pl.when(yl == 0)
    def _():
        mine[...] = fa[...] + ga[...].astype(F32)
        theirs[...] = (fb[...] + gb[...].astype(F32)).astype(BF)

    @pl.when(yl == 1)
    def _():
        mine[...] = fb[...] + gb[...].astype(F32)
        theirs[...] = (fa[...] + ga[...].astype(F32)).astype(BF)


def finish_encoder_body(idx, mine, theirs, out):
    out[0] = (mine[...] + theirs[...].astype(F32)).T.astype(BF)


def on_device(encoder_out, w_key, w_value, queries, grad_context):
    idx = jnp.zeros((8, 128), jnp.int32)
    c = lax.axis_index("seq") & 1
    qg_block = arr((272, 512))

    halves = jnp.stack([encoder_out[0, :, :256], encoder_out[0, :, 256:]])
    mine = lax.dynamic_index_in_dim(halves, c, 0, keepdims=False)
    other = lax.dynamic_index_in_dim(halves, 1 - c, 0, keepdims=False)
    from_y = [mine] + [swap_y(mine, m) for m in (1, 2, 3)]
    from_z = [other] + [swap_z(other, m) for m in (1, 2, 3)]
    idx, zb = call(join_z_body, "join_z", [idx, *from_z], [arr((1040, 256))], flops=10_000_000_000)
    idx, ya, qg0, qg_send = call(
        join_y_body, "join_y", [idx, *from_y, queries, grad_context],
        [arr((2, 512, 256)), qg_block, qg_block], flops=30_000_000_000,
    )
    by1, by3 = swap_y(zb, 1), swap_y(zb, 3)
    az1, az3 = swap_z(ya, 1), swap_z(ya, 3)
    by20, by21 = swap_y(by1[:528], 3), swap_y(by3[512:1040], 1)
    az20, az21 = swap_z(az1[:1], 3), swap_z(az3[1:], 1)

    ws = [w_key, w_value]
    qg2 = swap_seq(qg_send, 2)
    idx, acc, es = call(
        project_first_body, "project_first", [idx, *ws, ya, zb, by1, by3],
        [arr((512, 1024), F32), arr((4096, 256))],
    )
    idx, acc = call(
        project_next_body, "project_next", [idx, *ws, acc, az1, az3], [arr((512, 1024), F32)]
    )
    idx, kv_send, kv_own = call(
        project_last_body, "project_last", [idx, *ws, acc, by20, by21, az20, az21, qg0, qg2],
        [arr((768, 512)), arr((512, 512))],
    )
    kv_oth = swap_seq(kv_send, 1)
    idx, keep_t, es = call(
        turn_keep_body, "turn_keep", [idx, ya, az1, az20, az21, az3, by20, by21, es],
        [arr((8, 256, 512)), arr((4096, 256))], alias={8: 2},
    )
    idx, es = call(relay_body, "relay_rows", [idx, es, kv_oth], [arr((4096, 256))], alias={1: 1})
    es_oth = swap_seq(es, 1)

    idx, g, g_far, gq_own, gq_far = call(
        attend_body, "attend", [idx, kv_own, kv_oth, qg0, qg2],
        [arr((2304, 256)), arr((2, 512, 256)), arr((128, 256)), arr((128, 256))],
        [pltpu.VMEM((1024, 512), BF)] * 2,
    )
    gp = swap_seq(g, 1)
    far = swap_seq(g_far, 2)
    idx, oth_t = call(turn_other_body, "turn_other", [idx, es_oth], [arr((8, 256, 512))])

    one, two = (256, 512), (2, 256, 512)
    mats = [keep_t, oth_t, g, gp]
    idx, s1k, s1v = call(weights_first_body, "weights_first", [idx, *mats], [arr(two)] * 2)
    got1k, got1v = swap_x(s1k, 1), swap_x(s1v, 3)
    idx, s2k, s2v, k1k, k1v, k2k, k2v = call(
        weights_rest_body, "weights_rest", [idx, *mats], [arr(two)] * 2 + [arr(two, F32)] * 4
    )

    one_t, two_t = (512, 256), (2, 512, 256)
    rhs = [pltpu.VMEM((2048, 256), BF)]
    rhs_half = [pltpu.VMEM((1024, 256), BF)]
    idx, own = call(
        encoder_own_body, "encoder_own", [idx, *ws, g, gp], [arr((2, *two_t), F32)], rhs_half
    )
    idx, far = call(relay_body, "relay", [idx, far], [arr((2, 512, 256))], alias={1: 1})
    far_core = swap_seq(far[1:], 1)
    idx, ea, eb = call(
        encoder_sent_body, "encoder_sent", [idx, *ws, own, far, far_core], [arr(two_t)] * 2, rhs_half
    )
    got_a, got_b = swap_z(ea, 1), swap_z(eb, 3)
    idx, x1k, x1v, f1k, f1v = call(
        add_body, "add_first", [idx, k1k, k1v, got1k, got1v], [arr(one)] * 2 + [arr(one, F32)] * 2
    )
    last1k, last1v = swap_x(x1k, 3), swap_x(x1v, 1)
    idx, ka, kb = call(
        encoder_kept_body, "encoder_kept",
        [idx, *ws, g, gp, far, far_core], [arr(two_t, F32)] * 2, rhs,
    )
    idx, pair, s2k, s2v = call(
        pair_body, "weights_pair", [idx, f1k, f1v, last1k, last1v, gq_far, gp, s2k, s2v],
        [arr((640, 512)), arr(two), arr(two)], alias={7: 2, 8: 3},
    )
    w_theirs = swap_seq(pair, 2)
    got2k, got2v = swap_x(s2k, 1), swap_x(s2v, 3)
    idx, xa, xb, fa, fb = call(
        add_body, "encoder_add", [idx, ka, kb, got_a, got_b], [arr(one_t)] * 2 + [arr(one_t, F32)] * 2
    )
    last_a, last_b = swap_z(xa, 3), swap_z(xb, 1)
    idx, x2k, x2v, f2k, f2v = call(
        add_body, "weights_add", [idx, k2k, k2v, got2k, got2v], [arr(one)] * 2 + [arr(one, F32)] * 2
    )
    last2k, last2v = swap_x(x2k, 3), swap_x(x2v, 1)
    idx, e_mine, e_theirs = call(
        encoder_pair_body, "encoder_pair", [idx, fa, fb, last_a, last_b, w_theirs], [arr(one_t, F32), arr(one_t)]
    )
    e_got = swap_ylo(e_theirs)
    idx, grad_wk, grad_wv, grad_q = call(
        finish_weights_body, "finish_weights",
        [idx, f2k, f2v, last2k, last2v, w_theirs, gq_own, gp],
        [arr(two)] * 2 + [arr((2, 1, 128, 512))],
    )
    idx, grad_enc = call(finish_encoder_body, "finish_encoder", [idx, e_mine, e_got], [arr((1, 256, 512))])
    return grad_q, grad_enc, grad_wk, grad_wv


def solution(mesh):
    placed = (
        P("dp", "seq", "tensor"),
        P(None, None, "tensor"),
        P(None, None, "tensor"),
        P(None, "dp", "seq", "tensor"),
        P(None, "dp", "seq", "tensor"),
    )
    return jax.shard_map(
        on_device,
        mesh=mesh,
        in_specs=placed,
        out_specs=(
            P(None, "dp", "seq", "tensor"),
            P("dp", "seq", "tensor"),
            P(None, ("dp", "seq"), "tensor"),
            P(None, ("dp", "seq"), "tensor"),
        ),
        check_vma=False,
    )
```
